256 devices in a mesh: tile: 128 (over y, x, z_lo, core), mp: 2 (over z_hi).
Axes of the slice: x: 4, y: 4, z: 8 (z_hi: 2, z_lo: 4; z = z_hi * 4 + z_lo), core: 2. Of those that a mesh axis runs over, the one named last changes fastest.
Arguments:
- feat_cot: bfloat16 [512, 1024, 128], P(None, 'tile'), may hold values from -6 to 6
- latent: bfloat16 [16, 1024, 128], P(None, 'tile'), may hold values from -6 to 6
- dec_w1: bfloat16 [9, 512, 16], replicated, may hold values from -0.5 to 0.5
- dec_w2: bfloat16 [9, 512, 512], replicated, may hold values from -0.09375 to 0.09375
- hidden: bfloat16 [32768, 3072], P('tile', 'mp'), may hold values from -840 to 840
- modulation: bfloat16 [16, 2, 3072], P(None, None, 'mp'), may hold values from -3 to 3
- prompt_ids: int32 [8], replicated, may hold values from 0 to 15
- step_size: float32 [8], replicated, may hold values from 0.1 to 1
- proj_w: bfloat16 [3072, 64], P('mp'), may hold values from -0.75 to 0.75
Outputs:
- grad_hidden: bfloat16 [32768, 3072], P('tile', 'mp')
- grad_proj: float32 [3072, 64], P('mp')
- grad_mod: float32 [8, 2, 3072], P(None, None, 'mp')
The draws below stay inside these ranges and needn't reach their ends.
All inputs are finite; a program needn't handle non-finite values.
Results may differ from the reference program's by a relative error of at most 0.008.
Values may be sent and summed in bfloat16 or wider, within the bound.
No kernel may reach another device: no remote copies, remote signals or barrier semaphores. Data moves between devices by JAX's collectives and lax.ppermute only.
A program may use at most 128 MiB of HBM per device.

```python
import math
import jax
import jax.numpy as jnp
from jax import lax

LS = 128
LC = 16
C1 = 512
DD = 3072
PROMPTS = 16
IMGS = 8
H_ALL = 1024
PATCH_CH = 64
TOKENS = 32768


def draw_hidden(key, part):
    key_base, key_rows, key_cols = jax.random.split(key, 3)
    base = jnp.clip(jax.random.normal(key_base, (TOKENS, DD), jnp.float32), -6.0, 6.0)
    row_scale = jnp.exp(jax.random.uniform(key_rows, (TOKENS, 1), jnp.float32) * math.log(10.0))
    col_scale = jnp.exp(jax.random.uniform(key_cols, (1, DD), jnp.float32) * math.log(10.0))
    return (base * row_scale * col_scale).astype(jnp.bfloat16)


def place_ends(drawn, key, least, high):
    shape = drawn.shape
    spot = [jax.random.randint(jax.random.fold_in(key, axis), (), 0, shape[axis]) for axis in range(len(shape))]
    drawn = drawn.at[tuple(spot)].set(least)
    longest = shape.index(max(shape))
    spot[longest] = (spot[longest] + 1) % shape[longest]
    return drawn.at[tuple(spot)].set(high)


def block_levels(key, dims, cuts, low, top_value):
    def one(axis_at, blocks):
        steps = jax.random.uniform(jax.random.fold_in(jax.random.fold_in(key, 6), axis_at), (blocks,), jnp.float32, low / len(cuts), top_value / len(cuts))
        return jnp.repeat(jnp.exp(steps), dims[axis_at] // blocks).reshape((-1,) + (1,) * (len(dims) - axis_at - 1))

    factor_of = one(*cuts[0])
    for cut in cuts[1:]:
        factor_of = factor_of * one(*cut)
    return factor_of


def scatter_about(stream_key, extent, scale, limit, cuts=(), held_as=jnp.bfloat16):
    values = scale * jax.random.normal(stream_key, extent, jnp.float32)
    if cuts:
        values = values * block_levels(stream_key, extent, cuts, -0.22, 0.18)
    return jnp.clip(values, -limit, limit).astype(held_as)


def setup_inputs(seed: int = 0) -> dict:
    seeds = jax.random.split(jax.random.key(seed), 10)
    return {
        "feat_cot": scatter_about(seeds[0], (C1, H_ALL, LS), 1.0, 6.0, ((1, 128),)),
        "latent": scatter_about(seeds[1], (LC, H_ALL, LS), 1.0, 6.0, ((1, 128),)),
        "dec_w1": scatter_about(seeds[2], (9, C1, LC), (9 * LC) ** -0.5, 0.5),
        "dec_w2": scatter_about(seeds[3], (9, C1, C1), (9 * C1) ** -0.5, 0.09375),
        "hidden": draw_hidden(jax.random.fold_in(seeds[9], 71), 0),
        "modulation": scatter_about(seeds[5], (PROMPTS, 2, DD), 0.5, 3.0, ((2, 2),)),
        "prompt_ids": place_ends(jax.random.randint(seeds[6], (IMGS,), 0, PROMPTS), jax.random.fold_in(seeds[6], 1), 0, PROMPTS - 1).astype(jnp.int32),
        "step_size": jnp.clip(jnp.exp(jax.random.uniform(seeds[7], (IMGS,), jnp.float32, math.log(0.1), math.log(1.0))), 0.1, 1.0),
        "proj_w": scatter_about(seeds[8], (DD, PATCH_CH), PATCH_CH ** -0.5, 0.75, ((0, 2),)),
    }


def silu_grad(values):
    sigm = jax.nn.sigmoid(values)
    return sigm * (1.0 + values * (1.0 - sigm))

def conv_forward(source, weight):
    height, width = (source.shape[1], source.shape[2])
    padded = jnp.pad(source, ((0, 0), (1, 1), (1, 1)))
    result = jnp.zeros((weight.shape[1], height, width), jnp.float32)
    for kernel_tap in range(9):
        row_off, col_off = (kernel_tap // 3, kernel_tap % 3)
        result = result + jnp.einsum('oc,chw->ohw', weight[kernel_tap], padded[:, row_off:row_off + height, col_off:col_off + width])
    return result

def conv_backward(cotan, weight):
    height, width = (cotan.shape[1], cotan.shape[2])
    padded = jnp.pad(cotan, ((0, 0), (1, 1), (1, 1)))
    result = jnp.zeros((weight.shape[2], height, width), jnp.float32)
    for kernel_tap in range(9):
        row_off, col_off = (kernel_tap // 3, kernel_tap % 3)
        result = result + jnp.einsum('oc,ohw->chw', weight[kernel_tap], padded[:, 2 - row_off:2 - row_off + height, 2 - col_off:2 - col_off + width])
    return result

def reference(feat_cot, latent, dec_w1, dec_w2, hidden, modulation, prompt_ids, step_size, proj_w):
    row_shift = LS // 2
    token_shift = LS * LS // 8
    latent_images = jnp.roll(latent, row_shift, axis=1).reshape(LC, IMGS, LS, LS).transpose(1, 0, 2, 3)
    cot_images = jnp.roll(feat_cot, row_shift, axis=1).reshape(C1, IMGS, LS, LS).transpose(1, 0, 2, 3)
    hidden_images = jnp.roll(hidden, token_shift, axis=0).reshape(IMGS, TOKENS // IMGS, DD)
    weight_one = dec_w1.astype(jnp.float32)
    weight_two = dec_w2.astype(jnp.float32)
    half_side = LS // 2

    def one_image(packed):
        cot_one, latent_one, hidden_one, prompt_one, step_one = packed
        pre_one = conv_forward(latent_one.astype(jnp.float32), weight_one)
        act_one = jax.nn.silu(pre_one).astype(jnp.bfloat16)
        pre_two = conv_forward(act_one.astype(jnp.float32), weight_two)
        grad_two = (cot_one.astype(jnp.float32) * silu_grad(pre_two)).astype(jnp.bfloat16)
        grad_one = (conv_backward(grad_two.astype(jnp.float32), weight_two) * silu_grad(pre_one)).astype(jnp.bfloat16)
        grad_latent = conv_backward(grad_one.astype(jnp.float32), weight_one)
        tokens_grad = grad_latent.reshape(LC, half_side, 2, half_side, 2).transpose(1, 3, 0, 2, 4).reshape(half_side * half_side, 4 * LC)
        grad_velocity = (tokens_grad * -step_one).astype(jnp.bfloat16)
        states = hidden_one.astype(jnp.float32)
        mean_val = lax.optimization_barrier(jnp.mean(states, axis=1))
        spread = lax.optimization_barrier(jnp.mean(states * states, axis=1)) - mean_val * mean_val
        sigma = jnp.sqrt(spread + 1e-06)
        normed = (states - mean_val[:, None]) / sigma[:, None]
        mod_now = modulation[prompt_one].astype(jnp.float32)
        modulated = (normed * (1.0 + mod_now[1]) + mod_now[0]).astype(jnp.bfloat16)
        proj_part = jnp.dot(modulated.T, grad_velocity, preferred_element_type=jnp.float32)
        grad_modulated = jnp.dot(grad_velocity, proj_w.T, preferred_element_type=jnp.float32)
        mod_part = jnp.stack([lax.optimization_barrier(jnp.sum(grad_modulated, axis=0)), lax.optimization_barrier(jnp.sum(grad_modulated * normed, axis=0))])
        grad_normed = grad_modulated * (1.0 + mod_now[1])
        first_mean = lax.optimization_barrier(jnp.mean(grad_normed, axis=1))
        second_mean = lax.optimization_barrier(jnp.mean(grad_normed * normed, axis=1))
        grad_rows = ((grad_normed - first_mean[:, None] - normed * second_mean[:, None]) / sigma[:, None]).astype(jnp.bfloat16)
        return (grad_rows, proj_part, mod_part)
    grads, projs, mods = lax.map(one_image, (cot_images, latent_images, hidden_images, prompt_ids, step_size))
    grad_hidden = jnp.roll(grads.reshape(TOKENS, DD), -token_shift, axis=0)
    return (grad_hidden, lax.optimization_barrier(jnp.sum(projs, axis=0)), mods)
```

```python
import jax
import jax.numpy as jnp
from jax import lax
from jax.sharding import Mesh, PartitionSpec as P

BF = jnp.bfloat16
F32 = jnp.float32
TILE = ("y", "x", "zl", "core")


def padded_2(block, sides, width):
    for axis, dim in sides:
        count = lax.axis_size(axis)
        forward = [(i, i + 1) for i in range(count - 1)]
        forward.append((count - 1, 0))
        backward = [(target, source) for source, target in forward]
        low = lax.ppermute(
            lax.slice_in_dim(block, block.shape[dim] - width, None, axis=dim), axis, forward
        )
        high = lax.ppermute(lax.slice_in_dim(block, 0, width, axis=dim), axis, backward)
        block = jnp.concatenate([low, block, high], axis=dim)
    return block


def silu_grad(values):
    sigm = jax.nn.sigmoid(values)
    return sigm * (1.0 + values * (1.0 - sigm))


def conv_forward(padded, weight):
    out_rows = padded.shape[1] - 2
    width = padded.shape[2]
    widened = jnp.pad(padded, ((0, 0), (0, 0), (1, 1)))
    result = jnp.zeros((weight.shape[1], out_rows, width), F32)
    for kernel_tap in range(9):
        row_off, col_off = (kernel_tap // 3, kernel_tap % 3)
        result = result + jnp.einsum(
            "oc,crw->orw",
            weight[kernel_tap],
            widened[:, row_off : row_off + out_rows, col_off : col_off + width],
            preferred_element_type=F32,
        )
    return result


def conv_backward(padded, weight):
    out_rows = padded.shape[1] - 2
    width = padded.shape[2]
    widened = jnp.pad(padded, ((0, 0), (0, 0), (1, 1)))
    result = jnp.zeros((weight.shape[2], out_rows, width), F32)
    for kernel_tap in range(9):
        row_off, col_off = (kernel_tap // 3, kernel_tap % 3)
        result = result + jnp.einsum(
            "oc,orw->crw",
            weight[kernel_tap],
            widened[:, 2 - row_off : 2 - row_off + out_rows, 2 - col_off : 2 - col_off + width],
            preferred_element_type=F32,
        )
    return result


def keep_rows(values, extent, own_rows, image_side):
    row_start = (lax.axis_index(TILE) * own_rows + image_side // 2) % image_side
    position = row_start - extent + jnp.arange(values.shape[1])
    inside = (position >= 0) & (position < image_side)
    return jnp.where(inside[None, :, None], values, jnp.zeros((), values.dtype))


def sum_over_tile(part):
    half = part.shape[1] // 2
    core = lax.axis_index("core")
    swap = [(0, 1), (1, 0)]
    keep = lax.dynamic_slice_in_dim(part, core * half, half, 1)
    send = lax.dynamic_slice_in_dim(part, (1 - core) * half, half, 1)
    total = keep + lax.ppermute(send.astype(BF), "core", swap).astype(F32)
    for axis in ("zl", "x", "y"):
        count = lax.axis_size(axis)
        out = total.astype(BF)
        came = [
            lax.ppermute(out, axis, [(i, (i + d) % count) for i in range(count)])
            for d in range(1, count)
        ]
        for block in came:
            total = total + block.astype(F32)
    mine = total.astype(BF)
    other = lax.ppermute(mine, "core", swap)
    return jnp.where(
        core == 0,
        jnp.concatenate([mine, other], axis=1),
        jnp.concatenate([other, mine], axis=1),
    )


def body(feat_cot, latent, dec_w1, dec_w2, hidden, modulation, prompt_ids, step_size, proj_w):
    own_rows = latent.shape[1]
    image_side = latent.shape[2]
    channels = latent.shape[0]
    image_count = prompt_ids.shape[0]
    features = hidden.shape[1]
    image_index = (lax.axis_index(TILE) * own_rows + image_side // 2) // image_side % image_count
    image_hit = jnp.arange(image_count) == image_index
    image_pick = image_hit.astype(F32)
    step_now = jnp.sum(image_pick * step_size)
    prompt_now = jnp.sum(jnp.where(image_hit, prompt_ids, 0))
    mod_now = lax.dynamic_index_in_dim(modulation, prompt_now, 0, False).astype(F32)
    gain = 1.0 + mod_now[1]

    states = hidden.astype(F32)
    w_gain = (gain[:, None] * proj_w.astype(F32)).astype(BF)
    cross = jnp.dot(hidden, w_gain, preferred_element_type=F32)
    w_sum = jnp.sum(w_gain.astype(F32), axis=0)
    stats = jnp.concatenate(
        [
            jnp.concatenate(
                [cross, jnp.sum(states, axis=1)[:, None], jnp.sum(states * states, axis=1)[:, None]], 1
            ),
            jnp.pad(w_sum, (0, 2))[None],
        ],
        0,
    )
    stats = stats + lax.ppermute(stats, "mp", [(0, 1), (1, 0)])
    width_all = lax.axis_size("mp") * features
    patch = proj_w.shape[1]
    mean_val = stats[:-1, patch] / width_all
    spread = stats[:-1, patch + 1] / width_all - mean_val * mean_val
    sigma = jnp.sqrt(spread + 1e-06)
    w_sum = stats[-1, :patch]
    cross = (stats[:-1, :patch] - mean_val[:, None] * w_sum[None]) / sigma[:, None]

    latent_pad = keep_rows(padded_2(latent, ((TILE, 1),), 1), 1, own_rows, image_side)
    pre_one = conv_forward(latent_pad, dec_w1)
    act_one = jax.nn.silu(pre_one).astype(BF)
    act_pad = keep_rows(padded_2(act_one, ((TILE, 1),), 1), 1, own_rows, image_side)
    pre_two = conv_forward(act_pad, dec_w2)
    grad_two = (feat_cot * silu_grad(pre_two)).astype(BF)
    grad_pad = keep_rows(padded_2(grad_two, ((TILE, 1),), 1), 1, own_rows, image_side)
    grad_one = (conv_backward(grad_pad, dec_w2) * silu_grad(pre_one)).astype(BF)
    inner_pad = keep_rows(padded_2(grad_one, ((TILE, 1),), 1), 1, own_rows, image_side)
    grad_latent = conv_backward(inner_pad, dec_w1)
    token_rows = own_rows // 2
    half_side = image_side // 2
    tokens_grad = (
        grad_latent.reshape(channels, token_rows, 2, half_side, 2)
        .transpose(1, 3, 0, 2, 4)
        .reshape(token_rows * half_side, 4 * channels)
    )
    grad_velocity = (tokens_grad * -step_now).astype(BF)

    normed = (states - mean_val[:, None]) / sigma[:, None]
    cross_grad = jnp.einsum("tp,td->pd", grad_velocity, normed.astype(BF), preferred_element_type=F32)
    gv_sum = jnp.sum(grad_velocity.astype(F32), axis=0)
    w_t = proj_w.T
    proj_part = cross_grad * gain + mod_now[0] * gv_sum[:, None]
    mod_part = image_pick[:, None] * jnp.sum(cross_grad * w_t.astype(F32), axis=0)
    sums = image_pick[:, None] * gv_sum[None]
    high = sums.astype(BF).astype(F32)
    sums = jnp.pad(
        jnp.stack([high, sums - high]).reshape(2, image_count * patch),
        ((0, 6), (0, features - image_count * patch)),
    )
    total = sum_over_tile(jnp.concatenate([proj_part, mod_part, sums], 0)).astype(F32)
    grad_proj = total[:patch].T
    sums = (total[patch + 8] + total[patch + 9])[: image_count * patch].reshape(image_count, patch)
    first = jnp.dot(sums, w_t.astype(F32), precision=lax.Precision.HIGHEST)
    grad_mod = jnp.stack([first, total[patch : patch + 8]], axis=1)

    wide = grad_velocity.astype(F32)
    first_mean = jnp.sum(wide * w_sum[None], axis=1) / width_all
    second_mean = jnp.sum(wide * cross, axis=1) / width_all
    grad_normed = jnp.dot(grad_velocity, w_t, preferred_element_type=F32) * gain
    grad_hidden = (
        (grad_normed - first_mean[:, None] - normed * second_mean[:, None]) / sigma[:, None]
    ).astype(BF)
    return (grad_hidden, grad_proj, grad_mod)


def solution(mesh):
    fine = Mesh(
        mesh.devices.reshape(4, 4, 4, 2, 2), ("y", "x", "zl", "core", "mp")
    )
    return jax.shard_map(
        body,
        mesh=fine,
        in_specs=(
            P(None, TILE, None),
            P(None, TILE, None),
            P(),
            P(),
            P(TILE, "mp"),
            P(None, None, "mp"),
            P(),
            P(),
            P("mp", None),
        ),
        out_specs=(P(TILE, "mp"), P("mp", None), P(None, None, "mp")),
        check_vma=False,
    )
```

```python
import functools

import jax
import jax.numpy as jnp
from jax import lax
from jax.experimental import pallas as pl
from jax.experimental.pallas import tpu as pltpu
from jax.sharding import Mesh, PartitionSpec as P

BF = jnp.bfloat16
F32 = jnp.float32
TILE = ("y", "x", "zl", "core")
RINGS = ("zl", "x", "y")
OVER_0 = (((0,), (0,)), ((), ()))
OVER_1 = (((1,), (1,)), ((), ()))
WHOLE = pl.BlockSpec(memory_space=pltpu.VMEM)
SCALARS = pl.BlockSpec(memory_space=pltpu.SMEM)


def dot(a, b, dims=(((1,), (0,)), ((), ()))):
    return lax.dot_general(a, b, dims, preferred_element_type=F32)


def before(v, axis):
    place = lax.broadcasted_iota(jnp.int32, v.shape, axis)
    return jnp.where(place == 0, 0.0, pltpu.roll(v, 1, axis))


def after(v, axis):
    n = v.shape[axis]
    place = lax.broadcasted_iota(jnp.int32, v.shape, axis)
    return jnp.where(place == n - 1, 0.0, pltpu.roll(v, n - 1, axis))


def sigmoid(h):
    return 0.5 + 0.5 * jnp.tanh(0.5 * h)


def convs_kernel(rows, width, flags, low, high, lat_own, cot_own, w1, w1t, w2_hbm, out,
                 w2, lats, acts, dsilu, grads, inner, sem):
    ch = lat_own.shape[1]
    load = pltpu.make_async_copy(w2_hbm, w2, sem)
    load.start()
    top, bottom, step = flags[0], flags[1], flags[2]

    def keep(row):
        return top if row < 0 else bottom if row >= rows else None

    def masked(v, row):
        k = keep(row)
        return v if k is None else v * k

    def lat_line(row):
        if 0 <= row < rows:
            return lat_own[row]
        halo, i = (low, row + 4) if row < 0 else (high, row - rows)
        return halo[2 * width :, i * width : (i + 1) * width]

    def cot_line(row):
        if 0 <= row < rows:
            return cot_own[row]
        halo, i = (low, row + 2) if row < 0 else (high, row - rows)
        return halo[i * width : (i + 1) * width, :]

    for i in range(rows + 8):
        row = i - 4
        v = masked(lat_line(row).astype(F32), row)
        lats[0, i] = before(v, 1).astype(BF)
        lats[1, i] = v.astype(BF)
        lats[2, i] = after(v, 1).astype(BF)

    def store3(ref, i, v):
        at = pl.ds(i * width, width)
        ref[0, at, :] = before(v, 0).astype(BF)
        ref[1, at, :] = v.astype(BF)
        ref[2, at, :] = after(v, 0).astype(BF)

    for i in range(rows + 6):
        row = i - 3
        taps = [lats[kx, i + ky] for ky in range(3) for kx in range(3)]
        pre = dot(jnp.concatenate(taps, 0), w1[...], OVER_0)
        s = sigmoid(pre)
        act = pre * s
        if -1 <= row <= rows:
            dsilu[pl.ds((row + 1) * width, width), :] = s * (1.0 + pre * (1.0 - s))
        store3(acts, i, masked(act.astype(BF).astype(F32), row))
    load.wait()

    per = 2
    for i in range(0, rows + 4, per):
        pre = None
        for ky in range(3):
            for kx in range(3):
                part = dot(acts[kx, pl.ds((i + ky) * width, per * width), :], w2[3 * ky + kx], OVER_1)
                pre = part if pre is None else pre + part
        s = sigmoid(pre)
        slope = s * (1.0 + pre * (1.0 - s))
        for j in range(per):
            row = i + j - 2
            cot = cot_line(row).astype(F32)
            g = masked(cot * slope[j * width : (j + 1) * width], row)
            store3(grads, i + j, g)

    for i in range(0, rows + 2, per):
        back = None
        for ky in range(3):
            for kx in range(3):
                part = dot(grads[2 - kx, pl.ds((i + 2 - ky) * width, per * width), :], w2[3 * ky + kx])
                back = part if back is None else back + part
        for j in range(per):
            at = pl.ds((i + j) * width, width)
            g = back[j * width : (j + 1) * width] * dsilu[at, :]
            inner[at, :] = masked(g, i + j - 1).astype(BF)

    taps = dot(w1t[...], inner[...], OVER_1)
    lines = []
    for row in range(rows):
        by_kx = []
        for kx in range(3):
            total = None
            for ky in range(3):
                k = 3 * ky + kx
                at = (row + 2 - ky) * width
                part = taps[k * ch : (k + 1) * ch, at : at + width]
                total = part if total is None else total + part
            by_kx.append(total)
        whole = after(by_kx[0], 1) + by_kx[1] + before(by_kx[2], 1)
        lines.append((whole * step).astype(BF))

    half = width // 2
    spot = lax.broadcasted_iota(jnp.int32, (2 * width, 2 * width), 0)
    goal = lax.broadcasted_iota(jnp.int32, (2 * width, 2 * width), 1)
    within = lax.rem(goal, width)
    pick = (lax.div(spot, width) == lax.div(within, half)) & (
        lax.rem(spot, width) == 2 * lax.rem(within, half) + lax.div(goal, width)
    )
    pick = jnp.where(pick, 1.0, 0.0).astype(BF)
    stacked = [
        jnp.concatenate([lines[4 * h + a], lines[4 * h + 2 + a]], 1)
        for h in range(rows // 4)
        for a in range(2)
    ]
    apart = dot(jnp.concatenate(stacked, 0), pick).astype(BF)
    for h in range(rows // 4):
        for a in range(2):
            for b in range(2):
                out[pl.ds((2 * a + b) * ch, ch), pl.ds(h * width, width)] = apart[
                    (2 * h + a) * ch : (2 * h + a + 1) * ch, b * width : (b + 1) * width
                ]


def shift_and_gain(places, mod):
    chosen = mod[places[0]].astype(F32)
    return chosen[0:1], 1.0 + chosen[1:2]


def stats_kernel(places, hidden, mod, wt, out):
    _, gain = shift_and_gain(places, mod)
    patch = wt.shape[0]
    tokens = hidden.shape[0]
    w_gain = (wt[...].astype(F32) * gain).astype(BF)
    out[...] = jnp.zeros_like(out)
    out[0:tokens, 0:patch] = dot(hidden[...], w_gain, OVER_1)
    states = hidden[...].astype(F32)
    out[0:tokens, patch : patch + 1] = jnp.sum(states, axis=1, keepdims=True)
    out[0:tokens, patch + 1 : patch + 2] = jnp.sum(states * states, axis=1, keepdims=True)
    out[tokens:, 0:patch] = dot(jnp.ones((8, wt.shape[1]), BF), w_gain, OVER_1)


def norm_of(width_all, patch, stats, stats_far, hidden):
    tokens = hidden.shape[0]
    both = stats[...] + stats_far[...]
    mean_val = both[0:tokens, patch : patch + 1] / width_all
    spread = both[0:tokens, patch + 1 : patch + 2] / width_all - mean_val * mean_val
    scale = 1.0 / jnp.sqrt(spread + 1e-06)
    w_sum = both[tokens : tokens + 1, 0:patch]
    cross = (both[0:tokens, 0:patch] - mean_val * w_sum) * scale
    return (hidden[...].astype(F32) - mean_val) * scale, scale, w_sum, cross


def sums_kernel(width_all, images, places, gvt, stats, stats_far, hidden, mod, wt, send, keep, held):
    patch = gvt.shape[0]
    shift, gain = shift_and_gain(places, mod)
    normed = norm_of(width_all, patch, stats, stats_far, hidden)[0]
    cross_grad = dot(gvt[...], normed.astype(BF))
    column = jnp.sum(gvt[...].astype(F32), axis=1, keepdims=True)
    held[0:patch, :] = cross_grad * gain + shift * column
    mod_row = jnp.sum(cross_grad * wt[...].astype(F32), axis=0, keepdims=True)
    image = places[1]
    spot = lax.broadcasted_iota(jnp.int32, (images, mod_row.shape[1]), 0)
    held[patch : patch + images, :] = jnp.where(spot == image, mod_row, 0.0)
    row = dot(jnp.ones((8, gvt.shape[1]), BF), gvt[...], OVER_1)
    held[patch + images :, :] = jnp.zeros((8, mod_row.shape[1]), F32)
    wide = jnp.concatenate([row] * images, 1)
    lane = lax.broadcasted_iota(jnp.int32, wide.shape, 1)
    held[patch + images :, 0 : images * patch] = jnp.where(lax.div(lane, patch) == image, wide, 0.0)
    half = keep.shape[1]
    core = places[2]
    keep[...] = held[:, pl.ds(pl.multiple_of(core * half, half), half)]
    send[...] = held[:, pl.ds(pl.multiple_of((1 - core) * half, half), half)].astype(BF)


def hidden_kernel(width_all, places, gvt, stats, stats_far, hidden, mod, wt, out):
    patch = gvt.shape[0]
    _, gain = shift_and_gain(places, mod)
    normed, scale, w_sum, cross = norm_of(width_all, patch, stats, stats_far, hidden)
    gv = gvt[...].astype(F32).T
    first = jnp.sum(gv * w_sum, axis=1, keepdims=True) / width_all
    second = jnp.sum(gv * cross, axis=1, keepdims=True) / width_all
    grad = dot(gv.astype(BF), wt[...]) * gain
    out[...] = ((grad - first - normed * second) * scale).astype(BF)


def last_kernel(images, places, mine, other, wt, proj, mod):
    patch = wt.shape[0]
    half = mine.shape[1]
    core = places[2]
    source = lax.broadcasted_iota(jnp.int32, (patch, patch), 0)
    target = lax.broadcasted_iota(jnp.int32, (patch, patch), 1)
    ch = patch // 4
    order = jnp.where(target == 4 * lax.rem(source, ch) + lax.div(source, ch), 1.0, 0.0).astype(BF)
    for block, place in ((mine, core), (other, 1 - core)):
        at = pl.ds(pl.multiple_of(place * half, half), half)
        proj[at, :] = dot(block[0:patch, :], order, OVER_0)
        mod[:, 1, at] = block[patch : patch + images, :].astype(F32)
    wide = images * patch
    tail = patch + images
    mine_sum = mine[patch:, 0:wide].astype(F32)[images : images + 1]
    other_sum = other[patch:, 0:wide].astype(F32)[images : images + 1]
    line = jnp.where(core == 0, mine_sum, other_sum)
    sums = jnp.concatenate([line[:, i * patch : (i + 1) * patch] for i in range(images)], 0)
    mod[:, 0, :] = dot(sums.astype(BF), wt[...])


def call(kernel, out_shape, n_in, cost, name, scratch=(), smem=1):
    return pl.pallas_call(
        kernel,
        out_shape=out_shape,
        in_specs=[SCALARS] * smem + [WHOLE] * (n_in - smem),
        out_specs=jax.tree.map(lambda _: WHOLE, out_shape),
        scratch_shapes=list(scratch),
        compiler_params=pltpu.CompilerParams(vmem_limit_bytes=24 * 2**20),
        cost_estimate=pl.CostEstimate(flops=cost[0], bytes_accessed=cost[1], transcendentals=0),
        name=name,
    )


def sum_over_rings(total):
    for axis in RINGS:
        count = lax.axis_size(axis)
        out = total.astype(BF)
        came = [
            lax.ppermute(out, axis, [(i, (i + d) % count) for i in range(count)])
            for d in range(1, count)
        ]
        for block in came:
            total = total + block.astype(F32)
    return total


def body(feat_cot, latent, dec_w1, dec_w2, hidden, modulation, prompt_ids, step_size, proj_w):
    ch, rows, width = latent.shape
    mid = dec_w2.shape[1]
    images = prompt_ids.shape[0]
    tokens, features = hidden.shape
    patch = proj_w.shape[1]
    width_all = lax.axis_size("mp") * features
    tile = lax.axis_index(TILE)
    core = lax.axis_index("core")

    lat_own = latent.transpose(1, 0, 2)
    cot_own = feat_cot.transpose(1, 2, 0)

    def pack(lat_part, cot_part):
        return jnp.concatenate([cot_part.reshape(2 * width, mid), lat_part.reshape(ch, 4 * width)], 0)

    count = lax.axis_size(TILE)
    up = [(i, (i + 1) % count) for i in range(count)]
    low = lax.ppermute(pack(latent[:, -4:], cot_own[-2:]), TILE, up)
    high = lax.ppermute(pack(latent[:, :4], cot_own[:2]), TILE, [(b, a) for a, b in up])

    row_start = (tile * rows + width // 2) % width
    image = (tile * rows + width // 2) // width % images
    places = jnp.stack([prompt_ids[image], image, core]).astype(jnp.int32)
    flags = jnp.stack(
        [(row_start > 0).astype(F32), (row_start + rows < width).astype(F32), -step_size[image]]
    )
    wt = proj_w.reshape(features, ch, 4).transpose(2, 1, 0).reshape(patch, features)

    stats = call(
        stats_kernel, jax.ShapeDtypeStruct((tokens + 8, 128), F32), 4, (10**8, 10**6), "stats"
    )(places, hidden, modulation, wt)
    stats_far = lax.ppermute(stats, "mp", [(0, 1), (1, 0)])

    w1 = dec_w1.transpose(0, 2, 1).reshape(9 * ch, mid)
    gvt = pl.pallas_call(
        functools.partial(convs_kernel, rows, width),
        out_shape=jax.ShapeDtypeStruct((4 * ch, tokens), BF),
        in_specs=[SCALARS] + [WHOLE] * 6 + [pl.BlockSpec(memory_space=pl.ANY)],
        out_specs=WHOLE,
        scratch_shapes=[
            pltpu.VMEM(dec_w2.shape, BF),
            pltpu.VMEM((3, rows + 8, ch, width), BF),
            pltpu.VMEM((3, (rows + 6) * width, mid), BF),
            pltpu.VMEM(((rows + 2) * width, mid), F32),
            pltpu.VMEM((3, (rows + 4) * width, mid), BF),
            pltpu.VMEM(((rows + 2) * width, mid), BF),
            pltpu.SemaphoreType.DMA,
        ],
        compiler_params=pltpu.CompilerParams(vmem_limit_bytes=48 * 2**20),
        cost_estimate=pl.CostEstimate(
            flops=14 * 10**9, bytes_accessed=8 * 10**6, transcendentals=2 * 10**6
        ),
        name="convs",
    )(flags, low, high, lat_own, cot_own, w1, w1, dec_w2)

    lines = patch + images + 8
    half = features // 2
    send, keep = call(
        functools.partial(sums_kernel, width_all, images),
        (jax.ShapeDtypeStruct((lines, half), BF), jax.ShapeDtypeStruct((lines, half), F32)),
        7,
        (10**8, 2 * 10**6),
        "sums",
        scratch=(pltpu.VMEM((lines, features), F32),),
    )(places, gvt, stats, stats_far, hidden, modulation, wt)
    swap = [(0, 1), (1, 0)]
    mine = sum_over_rings(keep + lax.ppermute(send, "core", swap).astype(F32)).astype(BF)
    other = lax.ppermute(mine, "core", swap)

    grad_hidden = call(
        functools.partial(hidden_kernel, width_all),
        jax.ShapeDtypeStruct((tokens, features), BF),
        7,
        (10**8, 2 * 10**6),
        "grad_hidden",
    )(places, gvt, stats, stats_far, hidden, modulation, wt)

    grad_proj, grad_mod = call(
        functools.partial(last_kernel, images),
        (
            jax.ShapeDtypeStruct((features, patch), F32),
            jax.ShapeDtypeStruct((images, 2, features), F32),
        ),
        4,
        (10**7, 10**6),
        "last",
    )(places, mine, other, wt)
    return (grad_hidden, grad_proj, grad_mod)


def solution(mesh):
    fine = Mesh(mesh.devices.reshape(4, 4, 4, 2, 2), ("y", "x", "zl", "core", "mp"))
    return jax.shard_map(
        body,
        mesh=fine,
        in_specs=(
            P(None, TILE, None),
            P(None, TILE, None),
            P(),
            P(),
            P(TILE, "mp"),
            P(None, None, "mp"),
            P(),
            P(),
            P("mp", None),
        ),
        out_specs=(P(TILE, "mp"), P("mp", None), P(None, None, "mp")),
        check_vma=False,
    )
```

```python
import functools

import jax
import jax.numpy as jnp
from jax import lax
from jax.experimental import pallas as pl
from jax.experimental.pallas import tpu as pltpu
from jax.sharding import Mesh, PartitionSpec as P

BF = jnp.bfloat16
F32 = jnp.float32
TILE = ("y", "x", "zl", "core")
RINGS = ("zl", "x", "y")
OVER_0 = (((0,), (0,)), ((), ()))
OVER_1 = (((1,), (1,)), ((), ()))
WHOLE = pl.BlockSpec(memory_space=pltpu.VMEM)
SCALARS = pl.BlockSpec(memory_space=pltpu.SMEM)


def dot(a, b, dims=(((1,), (0,)), ((), ()))):
    return lax.dot_general(a, b, dims, preferred_element_type=F32)


def before(v, axis):
    place = lax.broadcasted_iota(jnp.int32, v.shape, axis)
    return jnp.where(place == 0, 0.0, pltpu.roll(v, 1, axis))


def after(v, axis):
    n = v.shape[axis]
    place = lax.broadcasted_iota(jnp.int32, v.shape, axis)
    return jnp.where(place == n - 1, 0.0, pltpu.roll(v, n - 1, axis))


def sigmoid(h):
    return 0.5 + 0.5 * jnp.tanh(0.5 * h)


def put_beside(ref, i, v):
    at = pl.ds(i * v.shape[0], v.shape[0])
    ref[0, at, :] = before(v, 0).astype(BF)
    ref[1, at, :] = v.astype(BF)
    ref[2, at, :] = after(v, 0).astype(BF)


def keeper(rows, width, images):
    row_start = place_of(rows, width, images)[1]
    top = jnp.where(row_start > 0, 1.0, 0.0)
    bottom = jnp.where(row_start + rows < width, 1.0, 0.0)

    def masked(v, row):
        return v * top if row < 0 else v * bottom if row >= rows else v

    return masked


def line_of(low, own, high, row):
    if row < 0:
        return low[low.shape[0] + row]
    return own[row] if row < own.shape[0] else high[row - own.shape[0]]


def forward_kernel(geometry, lat_low, lat_own, lat_high, w1, w2_far, slope_two, slope_one, lats, acts,
                   w2, sem):
    rows, width, _ = geometry
    load = pltpu.make_async_copy(w2_far, w2, sem)
    load.start()
    masked = keeper(*geometry)
    for i in range(rows + 8):
        row = i - 4
        v = masked(line_of(lat_low, lat_own, lat_high, row).astype(F32), row)
        lats[0, i] = before(v, 1).astype(BF)
        lats[1, i] = v.astype(BF)
        lats[2, i] = after(v, 1).astype(BF)

    for i in range(rows + 6):
        row = i - 3
        taps = [lats[kx, i + ky] for ky in range(3) for kx in range(3)]
        pre = dot(jnp.concatenate(taps, 0), w1[...], OVER_0)
        s = sigmoid(pre)
        if -1 <= row <= rows:
            slope_one[pl.ds((row + 1) * width, width), :] = s * (1.0 + pre * (1.0 - s))
        put_beside(acts, i, masked((pre * s).astype(BF).astype(F32), row))

    load.wait()
    per = 2
    for i in range(0, rows + 4, per):
        pre = None
        for ky in range(3):
            for kx in range(3):
                part = dot(acts[kx, pl.ds((i + ky) * width, per * width), :], w2[3 * ky + kx], OVER_1)
                pre = part if pre is None else pre + part
        s = sigmoid(pre)
        slope_two[pl.ds(i * width, per * width), :] = s * (1.0 + pre * (1.0 - s))


def backward_kernel(geometry, steps, slope_two, slope_one, cot_low, cot_own, cot_high, w1t, w2, out,
                    grads, inner):
    rows, width, _ = geometry
    ch = w1t.shape[0] // 9
    masked = keeper(*geometry)
    step = -steps[place_of(*geometry)[0]]
    for i in range(rows + 4):
        cot = line_of(cot_low, cot_own, cot_high, i - 2).astype(F32)
        g = masked(cot * slope_two[pl.ds(i * width, width), :], i - 2)
        put_beside(grads, i, g.astype(BF).astype(F32))

    per = 2
    for i in range(0, rows + 2, per):
        back = None
        for ky in range(3):
            for kx in range(3):
                part = dot(grads[2 - kx, pl.ds((i + 2 - ky) * width, per * width), :], w2[3 * ky + kx])
                back = part if back is None else back + part
        for j in range(per):
            at = pl.ds((i + j) * width, width)
            g = back[j * width : (j + 1) * width] * slope_one[at, :]
            inner[at, :] = masked(g, i + j - 1).astype(BF)

    taps = dot(w1t[...], inner[...], OVER_1)
    lines = []
    for row in range(rows):
        by_kx = []
        for kx in range(3):
            total = None
            for ky in range(3):
                k = 3 * ky + kx
                at = (row + 2 - ky) * width
                part = taps[k * ch : (k + 1) * ch, at : at + width]
                total = part if total is None else total + part
            by_kx.append(total)
        whole = after(by_kx[0], 1) + by_kx[1] + before(by_kx[2], 1)
        lines.append((whole * step).astype(BF))

    half = width // 2
    spot = lax.broadcasted_iota(jnp.int32, (2 * width, 2 * width), 0)
    goal = lax.broadcasted_iota(jnp.int32, (2 * width, 2 * width), 1)
    within = lax.rem(goal, width)
    pick = (lax.div(spot, width) == lax.div(within, half)) & (
        lax.rem(spot, width) == 2 * lax.rem(within, half) + lax.div(goal, width)
    )
    pick = jnp.where(pick, 1.0, 0.0).astype(BF)
    stacked = [
        jnp.concatenate([lines[4 * h + a], lines[4 * h + 2 + a]], 1)
        for h in range(rows // 4)
        for a in range(2)
    ]
    apart = dot(jnp.concatenate(stacked, 0), pick).astype(BF)
    by_tap = jnp.concatenate(
        [
            jnp.concatenate(
                [
                    apart[(2 * h + a) * ch : (2 * h + a + 1) * ch, b * width : (b + 1) * width]
                    for h in range(rows // 4)
                ],
                1,
            )
            for a in range(2)
            for b in range(2)
        ],
        0,
    )
    goal = lax.broadcasted_iota(jnp.int32, (4 * ch, 4 * ch), 0)
    spot = lax.broadcasted_iota(jnp.int32, (4 * ch, 4 * ch), 1)
    order = jnp.where(goal == 4 * lax.rem(spot, ch) + lax.div(spot, ch), 1.0, 0.0).astype(BF)
    out[...] = dot(order, by_tap).astype(BF)


def place_of(rows, width, images):
    tile = 0
    for axis in TILE:
        tile = tile * lax.axis_size(axis) + lax.axis_index(axis)
    row = tile * rows + width // 2
    return lax.rem(lax.div(row, width), images), lax.rem(row, width)


def shift_and_gain(prompt, mod):
    chosen = mod[prompt].astype(F32)
    return chosen[0:1], 1.0 + chosen[1:2]


def stats_kernel(geometry, prompts, hidden, mod, wt, out):
    _, gain = shift_and_gain(prompts[place_of(*geometry)[0]], mod)
    patch = wt.shape[0]
    tokens = hidden.shape[0]
    w_gain = (wt[...].astype(F32) * gain).astype(BF)
    out[...] = jnp.zeros_like(out)
    out[0:tokens, 0:patch] = dot(hidden[...], w_gain, OVER_1)
    states = hidden[...].astype(F32)
    out[0:tokens, patch : patch + 1] = jnp.sum(states, axis=1, keepdims=True)
    out[0:tokens, patch + 1 : patch + 2] = jnp.sum(states * states, axis=1, keepdims=True)
    out[tokens:, 0:patch] = dot(jnp.ones((8, wt.shape[1]), BF), w_gain, OVER_1)


def norm_of(width_all, patch, stats, stats_far, hidden):
    tokens = hidden.shape[0]
    both = stats[...] + stats_far[...]
    mean_val = both[0:tokens, patch : patch + 1] / width_all
    spread = both[0:tokens, patch + 1 : patch + 2] / width_all - mean_val * mean_val
    scale = 1.0 / jnp.sqrt(spread + 1e-06)
    w_sum = both[tokens : tokens + 1, 0:patch]
    cross = (both[0:tokens, 0:patch] - mean_val * w_sum) * scale
    return (hidden[...].astype(F32) - mean_val) * scale, scale, w_sum, cross


def sums_kernel(width_all, geometry, prompts, gvt, stats, stats_far, hidden, mod, wt, send, keep, held):
    patch = gvt.shape[0]
    image, images = place_of(*geometry)[0], geometry[2]
    shift, gain = shift_and_gain(prompts[image], mod)
    normed = norm_of(width_all, patch, stats, stats_far, hidden)[0]
    cross_grad = dot(gvt[...], normed.astype(BF))
    column = jnp.sum(gvt[...].astype(F32), axis=1, keepdims=True)
    held[0:patch, :] = cross_grad * gain + shift * column
    mod_row = jnp.sum(cross_grad * wt[...].astype(F32), axis=0, keepdims=True)
    spot = lax.broadcasted_iota(jnp.int32, (images, mod_row.shape[1]), 0)
    held[patch : patch + images, :] = jnp.where(spot == image, mod_row, 0.0)
    row = dot(jnp.ones((8, gvt.shape[1]), BF), gvt[...], OVER_1)
    held[patch + images :, :] = jnp.zeros((8, mod_row.shape[1]), F32)
    wide = jnp.concatenate([row] * images, 1)
    lane = lax.broadcasted_iota(jnp.int32, wide.shape, 1)
    held[patch + images :, 0 : images * patch] = jnp.where(lax.div(lane, patch) == image, wide, 0.0)
    half = keep.shape[1]
    core = lax.axis_index("core")
    keep[...] = held[:, pl.ds(pl.multiple_of(core * half, half), half)]
    send[...] = held[:, pl.ds(pl.multiple_of((1 - core) * half, half), half)].astype(BF)


def hidden_kernel(width_all, geometry, prompts, gvt, stats, stats_far, hidden, mod, wt, out):
    patch = gvt.shape[0]
    _, gain = shift_and_gain(prompts[place_of(*geometry)[0]], mod)
    normed, scale, w_sum, cross = norm_of(width_all, patch, stats, stats_far, hidden)
    gv = gvt[...].astype(F32).T
    first = jnp.sum(gv * w_sum, axis=1, keepdims=True) / width_all
    second = jnp.sum(gv * cross, axis=1, keepdims=True) / width_all
    grad = dot(gv.astype(BF), wt[...]) * gain
    out[...] = ((grad - first - normed * second) * scale).astype(BF)


def last_kernel(images, mine, other, wt, proj, mod):
    patch = wt.shape[0]
    half = mine.shape[1]
    core = lax.axis_index("core")
    for block, place in ((mine, core), (other, 1 - core)):
        at = pl.ds(pl.multiple_of(place * half, half), half)
        proj[:, at] = block[0:patch, :].astype(F32)
        mod[:, 1, at] = block[patch : patch + images, :].astype(F32)
    wide = images * patch
    mine_sum = mine[patch:, 0:wide].astype(F32)[images : images + 1]
    other_sum = other[patch:, 0:wide].astype(F32)[images : images + 1]
    line = jnp.where(core == 0, mine_sum, other_sum)
    sums = jnp.concatenate([line[:, i * patch : (i + 1) * patch] for i in range(images)], 0)
    mod[:, 0, :] = dot(sums.astype(BF), wt[...])


def call(kernel, out_shape, n_in, cost, name, scratch=(), smem=1, far=0):
    return pl.pallas_call(
        kernel,
        out_shape=out_shape,
        in_specs=[SCALARS] * smem + [WHOLE] * (n_in - smem - far) + [pl.BlockSpec(memory_space=pl.ANY)] * far,
        out_specs=jax.tree.map(lambda _: WHOLE, out_shape),
        scratch_shapes=list(scratch),
        compiler_params=pltpu.CompilerParams(vmem_limit_bytes=40 * 2**20),
        cost_estimate=pl.CostEstimate(flops=cost[0], bytes_accessed=cost[1], transcendentals=0),
        name=name,
    )


def sum_over_rings(total, beside):
    for axis in RINGS:
        count = lax.axis_size(axis)
        out = total.astype(BF)
        came = [
            lax.ppermute(out, axis, [(i, (i + d) % count) for i in range(count)])
            for d in range(1, count)
        ]
        if axis == RINGS[0]:
            came, beside = lax.optimization_barrier((came, beside))
        for block in came:
            total = total + block.astype(F32)
    return total, beside


def body(feat_cot, latent, dec_w1, dec_w2, hidden, modulation, prompt_ids, step_size, proj_w):
    ch, rows, width = latent.shape
    mid = dec_w2.shape[1]
    images = prompt_ids.shape[0]
    tokens, features = hidden.shape
    patch = proj_w.shape[1]
    width_all = lax.axis_size("mp") * features
    geometry = (rows, width, images)
    count = lax.axis_size(TILE)
    up = [(i, (i + 1) % count) for i in range(count)]
    down = [(b, a) for a, b in up]

    lat_own = lax.optimization_barrier(latent.transpose(1, 0, 2))
    lat_low = lax.ppermute(lat_own[-4:], TILE, up)
    lat_high = lax.ppermute(lat_own[:4], TILE, down)
    cot_own = lax.optimization_barrier(feat_cot.transpose(1, 2, 0))
    cot_low = lax.ppermute(cot_own[-2:], TILE, up)
    cot_high = lax.ppermute(cot_own[:2], TILE, down)
    wt = proj_w.T

    stats = call(
        functools.partial(stats_kernel, geometry),
        jax.ShapeDtypeStruct((tokens + 8, 128), F32),
        4,
        (10**8, 10**6),
        "stats",
    )(prompt_ids, hidden, modulation, wt)
    stats_far = lax.ppermute(stats, "mp", [(0, 1), (1, 0)])

    w1 = dec_w1.transpose(0, 2, 1).reshape(9 * ch, mid)
    slope_two, slope_one = call(
        functools.partial(forward_kernel, geometry),
        (
            jax.ShapeDtypeStruct(((rows + 4) * width, mid), F32),
            jax.ShapeDtypeStruct(((rows + 2) * width, mid), F32),
        ),
        5,
        (8 * 10**9, 8 * 10**6),
        "forward",
        scratch=(
            pltpu.VMEM((3, rows + 8, ch, width), BF),
            pltpu.VMEM((3, (rows + 6) * width, mid), BF),
            pltpu.VMEM(dec_w2.shape, BF),
            pltpu.SemaphoreType.DMA,
        ),
        smem=0,
        far=1,
    )(lat_low, lat_own, lat_high, w1, dec_w2)
    gvt = call(
        functools.partial(backward_kernel, geometry),
        jax.ShapeDtypeStruct((4 * ch, tokens), BF),
        8,
        (7 * 10**9, 8 * 10**6),
        "backward",
        scratch=(
            pltpu.VMEM((3, (rows + 4) * width, mid), BF),
            pltpu.VMEM(((rows + 2) * width, mid), BF),
        ),
    )(step_size, slope_two, slope_one, cot_low, cot_own, cot_high, w1, dec_w2)

    lines = patch + images + 8
    half = features // 2
    send, keep = call(
        functools.partial(sums_kernel, width_all, geometry),
        (jax.ShapeDtypeStruct((lines, half), BF), jax.ShapeDtypeStruct((lines, half), F32)),
        7,
        (10**8, 2 * 10**6),
        "sums",
        scratch=(pltpu.VMEM((lines, features), F32),),
    )(prompt_ids, gvt, stats, stats_far, hidden, modulation, wt)
    grad_hidden = call(
        functools.partial(hidden_kernel, width_all, geometry),
        jax.ShapeDtypeStruct((tokens, features), BF),
        7,
        (10**8, 2 * 10**6),
        "grad_hidden",
    )(prompt_ids, gvt, stats, stats_far, hidden, modulation, wt)

    swap = [(0, 1), (1, 0)]
    total, grad_hidden = sum_over_rings(
        keep + lax.ppermute(send, "core", swap).astype(F32), grad_hidden
    )
    mine = total.astype(BF)
    other = lax.ppermute(mine, "core", swap)

    grad_proj, grad_mod = call(
        functools.partial(last_kernel, images),
        (
            jax.ShapeDtypeStruct((patch, features), F32),
            jax.ShapeDtypeStruct((images, 2, features), F32),
        ),
        3,
        (10**7, 10**6),
        "last",
        smem=0,
    )(mine, other, wt)
    return (grad_hidden, grad_proj.T, grad_mod)


def solution(mesh):
    fine = Mesh(mesh.devices.reshape(4, 4, 4, 2, 2), ("y", "x", "zl", "core", "mp"))
    return jax.shard_map(
        body,
        mesh=fine,
        in_specs=(
            P(None, TILE, None),
            P(None, TILE, None),
            P(),
            P(),
            P(TILE, "mp"),
            P(None, None, "mp"),
            P(),
            P(),
            P("mp", None),
        ),
        out_specs=(P(TILE, "mp"), P("mp", None), P(None, None, "mp")),
        check_vma=False,
    )
```

```python
import functools

import jax
import jax.numpy as jnp
from jax import lax
from jax.experimental import pallas as pl
from jax.experimental.pallas import tpu as pltpu
from jax.sharding import Mesh, PartitionSpec as P

BF = jnp.bfloat16
F32 = jnp.float32
TILE = ("y", "x", "zl", "core")
OVER_0 = (((0,), (0,)), ((), ()))
OVER_1 = (((1,), (1,)), ((), ()))
WHOLE = pl.BlockSpec(memory_space=pltpu.VMEM)
SCALARS = pl.BlockSpec(memory_space=pltpu.SMEM)


def dot(a, b, dims=(((1,), (0,)), ((), ()))):
    return lax.dot_general(a, b, dims, preferred_element_type=F32)


def before(v, axis):
    place = lax.broadcasted_iota(jnp.int32, v.shape, axis)
    return jnp.where(place == 0, 0.0, pltpu.roll(v, 1, axis))


def after(v, axis):
    n = v.shape[axis]
    place = lax.broadcasted_iota(jnp.int32, v.shape, axis)
    return jnp.where(place == n - 1, 0.0, pltpu.roll(v, n - 1, axis))


def sigmoid(h):
    return 0.5 + 0.5 * jnp.tanh(0.5 * h)


def put_beside(ref, i, v, cols):
    at = pl.ds(i * v.shape[0], v.shape[0])
    ref[0, at, cols] = before(v, 0).astype(BF)
    ref[1, at, cols] = v.astype(BF)
    ref[2, at, cols] = after(v, 0).astype(BF)


def keeper(rows, width, images):
    row_start = place_of(rows, width, images)[1]
    top = jnp.where(row_start > 0, 1.0, 0.0)
    bottom = jnp.where(row_start + rows < width, 1.0, 0.0)

    def masked(v, row):
        return v * top if row < 0 else v * bottom if row >= rows else v

    return masked


def line_of(low, own, high, row):
    if row < 0:
        return low[low.shape[0] + row]
    return own[row] if row < own.shape[0] else high[row - own.shape[0]]


def conv_tile(tap, meanwhile):
    total = None
    for k in range(9):
        part = tap(k)
        total = part if total is None else total + part
        for step in meanwhile[k::9]:
            step()
    return total


def forward_kernel(geometry, lat_low, lat_own, lat_high, w1, w2_far, slope_two, slope_one, lats, acts,
                   w2, sems):
    rows, width, _ = geometry
    loads = [pltpu.make_async_copy(w2_far.at[k], w2.at[k], sems.at[k]) for k in range(9)]
    for load in loads:
        load.start()
    masked = keeper(*geometry)
    for i in range(rows + 8):
        row = i - 4
        v = masked(line_of(lat_low, lat_own, lat_high, row).astype(F32), row)
        lats[0, i] = before(v, 1).astype(BF)
        lats[1, i] = v.astype(BF)
        lats[2, i] = after(v, 1).astype(BF)
    mid = w1.shape[1]
    part_width = mid // 2
    halves = [slice(0, part_width), slice(part_width, mid)]

    def first_layer(i, cols):
        row = i - 3
        taps = [lats[kx, i + ky] for ky in range(3) for kx in range(3)]
        pre = dot(jnp.concatenate(taps, 0), w1[:, cols], OVER_0)
        s = sigmoid(pre)
        if -1 <= row <= rows:
            slope_one[pl.ds((row + 1) * width, width), cols] = s * (1.0 + pre * (1.0 - s))
        put_beside(acts, i, masked((pre * s).astype(BF).astype(F32), row), cols)

    def finish(i, pre, j, cols):
        h = pre[j * width : (j + 1) * width, cols]
        s = sigmoid(h)
        slope_two[pl.ds((i + j) * width, width), cols] = s * (1.0 + h * (1.0 - s))

    per = 2
    for i in range(per + 2):
        for cols in halves:
            first_layer(i, cols)
    steps = []
    for i in range(0, rows + 4, per):
        nexts = [
            functools.partial(first_layer, i + per + 2 + j, cols)
            for j in range(per)
            for cols in halves
            if i + per + 2 + j < rows + 6
        ]

        def tap(k):
            if i == 0:
                loads[k].wait()
            return dot(acts[k % 3, pl.ds((i + k // 3) * width, per * width), :], w2[k], OVER_1)

        pre = conv_tile(tap, nexts + steps)
        steps = [
            functools.partial(finish, i, pre, j, cols) for j in range(per) for cols in halves
        ]
    for step in steps:
        step()


def backward_kernel(geometry, steps, slope_two, slope_one, cot_low, cot_own, cot_high, w1t, w2, out,
                    grads, inner):
    rows, width, _ = geometry
    ch = w1t.shape[0] // 9
    mid = w2.shape[1]
    part_width = mid // 2
    halves = [slice(0, part_width), slice(part_width, mid)]
    masked = keeper(*geometry)
    step = -steps[place_of(*geometry)[0]]

    def second_grad(i, cols):
        cot = line_of(cot_low, cot_own, cot_high, i - 2)[:, cols].astype(F32)
        g = masked(cot * slope_two[pl.ds(i * width, width), cols], i - 2)
        put_beside(grads, i, g.astype(BF).astype(F32), cols)

    taps = []

    def finish(i, back, j, cols):
        at = pl.ds((i + j) * width, width)
        g = back[j * width : (j + 1) * width, cols] * slope_one[at, cols]
        inner[at, cols] = masked(g, i + j - 1).astype(BF)

    per = 2

    def first_taps(i):
        taps.append(dot(w1t[...], inner[pl.ds(i * width, per * width), :], OVER_1))

    for i in range(per + 2):
        for cols in halves:
            second_grad(i, cols)
    todo = []
    for i in range(0, rows + 2, per):
        nexts = [
            functools.partial(second_grad, i + per + 2 + j, cols)
            for j in range(per)
            for cols in halves
            if i + per + 2 + j < rows + 4
        ]

        def tap(k):
            at = pl.ds((i + 2 - k // 3) * width, per * width)
            return dot(grads[2 - k % 3, at, :], w2[k])

        back = conv_tile(tap, nexts + todo)
        todo = [functools.partial(finish, i, back, j, cols) for j in range(per) for cols in halves]
        todo.append(functools.partial(first_taps, i))
    for part in todo:
        part()
    taps = jnp.concatenate(taps, 1)

    lines = []
    for row in range(rows):
        by_kx = []
        for kx in range(3):
            total = None
            for ky in range(3):
                k = 3 * ky + kx
                at = (row + 2 - ky) * width
                part = taps[k * ch : (k + 1) * ch, at : at + width]
                total = part if total is None else total + part
            by_kx.append(total)
        whole = after(by_kx[0], 1) + by_kx[1] + before(by_kx[2], 1)
        lines.append((whole * step).astype(BF))

    half = width // 2
    spot = lax.broadcasted_iota(jnp.int32, (2 * width, 2 * width), 0)
    goal = lax.broadcasted_iota(jnp.int32, (2 * width, 2 * width), 1)
    within = lax.rem(goal, width)
    pick = (lax.div(spot, width) == lax.div(within, half)) & (
        lax.rem(spot, width) == 2 * lax.rem(within, half) + lax.div(goal, width)
    )
    pick = jnp.where(pick, 1.0, 0.0).astype(BF)
    stacked = [
        jnp.concatenate([lines[4 * h + a], lines[4 * h + 2 + a]], 1)
        for h in range(rows // 4)
        for a in range(2)
    ]
    apart = dot(jnp.concatenate(stacked, 0), pick).astype(BF)
    by_tap = jnp.concatenate(
        [
            jnp.concatenate(
                [
                    apart[(2 * h + a) * ch : (2 * h + a + 1) * ch, b * width : (b + 1) * width]
                    for h in range(rows // 4)
                ],
                1,
            )
            for a in range(2)
            for b in range(2)
        ],
        0,
    )
    goal = lax.broadcasted_iota(jnp.int32, (4 * ch, 4 * ch), 0)
    spot = lax.broadcasted_iota(jnp.int32, (4 * ch, 4 * ch), 1)
    order = jnp.where(goal == 4 * lax.rem(spot, ch) + lax.div(spot, ch), 1.0, 0.0).astype(BF)
    out[...] = dot(order, by_tap).astype(BF)


def place_of(rows, width, images):
    tile = 0
    for axis in TILE:
        tile = tile * lax.axis_size(axis) + lax.axis_index(axis)
    row = tile * rows + width // 2
    return lax.rem(lax.div(row, width), images), lax.rem(row, width)


def shift_and_gain(prompt, mod):
    chosen = mod[prompt].astype(F32)
    return chosen[0:1], 1.0 + chosen[1:2]


def stats_kernel(geometry, prompts, hidden, mod, wt, out):
    _, gain = shift_and_gain(prompts[place_of(*geometry)[0]], mod)
    patch = wt.shape[0]
    tokens = hidden.shape[0]
    w_gain = (wt[...].astype(F32) * gain).astype(BF)
    out[...] = jnp.zeros_like(out)
    out[0:tokens, 0:patch] = dot(hidden[...], w_gain, OVER_1)
    states = hidden[...].astype(F32)
    out[0:tokens, patch : patch + 1] = jnp.sum(states, axis=1, keepdims=True)
    out[0:tokens, patch + 1 : patch + 2] = jnp.sum(states * states, axis=1, keepdims=True)
    out[tokens:, 0:patch] = dot(jnp.ones((8, wt.shape[1]), BF), w_gain, OVER_1)


def norm_of(width_all, patch, stats, stats_far, hidden):
    tokens = hidden.shape[0]
    both = stats[...] + stats_far[...]
    mean_val = both[0:tokens, patch : patch + 1] / width_all
    spread = both[0:tokens, patch + 1 : patch + 2] / width_all - mean_val * mean_val
    scale = 1.0 / jnp.sqrt(spread + 1e-06)
    w_sum = both[tokens : tokens + 1, 0:patch]
    cross = (both[0:tokens, 0:patch] - mean_val * w_sum) * scale
    return (hidden[...].astype(F32) - mean_val) * scale, scale, w_sum, cross


def sums_kernel(width_all, geometry, prompts, gvt, stats, stats_far, hidden, mod, wt, send, keep, held):
    patch = gvt.shape[0]
    image, images = place_of(*geometry)[0], geometry[2]
    shift, gain = shift_and_gain(prompts[image], mod)
    normed = norm_of(width_all, patch, stats, stats_far, hidden)[0]
    cross_grad = dot(gvt[...], normed.astype(BF))
    column = jnp.sum(gvt[...].astype(F32), axis=1, keepdims=True)
    held[0:patch, :] = cross_grad * gain + shift * column
    mod_row = jnp.sum(cross_grad * wt[...].astype(F32), axis=0, keepdims=True)
    spot = lax.broadcasted_iota(jnp.int32, (images, mod_row.shape[1]), 0)
    held[patch : patch + images, :] = jnp.where(spot == image, mod_row, 0.0)
    row = dot(jnp.ones((8, gvt.shape[1]), BF), gvt[...], OVER_1)
    held[patch + images :, :] = jnp.zeros((8, mod_row.shape[1]), F32)
    wide = jnp.concatenate([row] * images, 1)
    lane = lax.broadcasted_iota(jnp.int32, wide.shape, 1)
    held[patch + images :, 0 : images * patch] = jnp.where(lax.div(lane, patch) == image, wide, 0.0)
    lines, count = held.shape[0], keep.shape[0] // held.shape[0]
    core = lax.axis_index("core")
    for j in range(count):
        at = pl.ds(j * lines, lines)
        for ref, side in ((keep, core), (send, 1 - core)):
            lanes = pl.ds(pl.multiple_of((side * count + j) * 128, 128), 128)
            ref[at, :] = held[:, lanes].astype(ref.dtype)


def hidden_kernel(width_all, geometry, prompts, gvt, stats, stats_far, hidden, mod, wt, out):
    patch = gvt.shape[0]
    _, gain = shift_and_gain(prompts[place_of(*geometry)[0]], mod)
    normed, scale, w_sum, cross = norm_of(width_all, patch, stats, stats_far, hidden)
    gv = gvt[...].astype(F32).T
    first = jnp.sum(gv * w_sum, axis=1, keepdims=True) / width_all
    second = jnp.sum(gv * cross, axis=1, keepdims=True) / width_all
    grad = dot(gv.astype(BF), wt[...]) * gain
    out[...] = ((grad - first - normed * second) * scale).astype(BF)


def last_kernel(images, mine, other, wt, proj, mod, held):
    patch = wt.shape[0]
    count, piece = mine.shape[0], mine.shape[1]
    lines = patch + images + 8
    core, zl = lax.axis_index("core"), lax.axis_index("zl")
    for d in range(count):
        at = pl.ds(pl.multiple_of(lax.rem(zl + d, count) * piece, 8), piece)
        held[core, at, :] = mine[d].astype(F32)
        held[1 - core, at, :] = other[d].astype(F32)
    blocks = count * piece // lines
    for side in range(2):
        for j in range(blocks):
            at = pl.ds((side * blocks + j) * 128, 128)
            proj[:, at] = held[side, pl.ds(j * lines, patch), :]
            mod[:, 1, at] = held[side, pl.ds(j * lines + patch, images), :]
    sums = []
    for i in range(images):
        j, lane = divmod(i * patch, 128)
        row = held[0, pl.ds(j * lines + patch + images, 1), :]
        sums.append(row[:, lane : lane + patch])
    mod[:, 0, :] = dot(jnp.concatenate(sums, 0).astype(BF), wt[...])


def call(kernel, out_shape, n_in, cost, name, scratch=(), smem=1, far=0, vmem=24):
    return pl.pallas_call(
        kernel,
        out_shape=out_shape,
        in_specs=[SCALARS] * smem + [WHOLE] * (n_in - smem - far) + [pl.BlockSpec(memory_space=pltpu.HBM)] * far,
        out_specs=jax.tree.map(lambda _: WHOLE, out_shape),
        scratch_shapes=list(scratch),
        compiler_params=pltpu.CompilerParams(vmem_limit_bytes=vmem * 2**20),
        cost_estimate=pl.CostEstimate(flops=cost[0], bytes_accessed=cost[1], transcendentals=0),
        name=name,
    )


def sum_over_chips(part, beside):
    count = lax.axis_size("zl")
    zl = lax.axis_index("zl")

    def piece(d):
        return lax.dynamic_index_in_dim(part, lax.rem(zl + d, count), 0, False)

    total = piece(0)
    came = [
        lax.ppermute(piece(d).astype(BF), "zl", [(i, (i + d) % count) for i in range(count)])
        for d in range(1, count)
    ]
    came, beside = lax.optimization_barrier((came, beside))
    for block in came:
        total = total + block.astype(F32)
    plane = ("y", "x")
    chips = lax.axis_size(plane)
    copies = jnp.broadcast_to(total.astype(BF)[None], (chips,) + total.shape)
    total = jnp.sum(lax.all_to_all(copies, plane, 0, 0).astype(F32), axis=0)
    total = lax.optimization_barrier(total).astype(BF)
    came = [
        lax.ppermute(total, "zl", [(i, (i - d) % count) for i in range(count)])
        for d in range(1, count)
    ]
    return jnp.stack([total] + came, 0), beside


def body(feat_cot, latent, dec_w1, dec_w2, hidden, modulation, prompt_ids, step_size, proj_w):
    ch, rows, width = latent.shape
    mid = dec_w2.shape[1]
    images = prompt_ids.shape[0]
    tokens, features = hidden.shape
    patch = proj_w.shape[1]
    width_all = lax.axis_size("mp") * features
    geometry = (rows, width, images)
    count = lax.axis_size(TILE)
    up = [(i, (i + 1) % count) for i in range(count)]
    down = [(b, a) for a, b in up]

    cot_own = lax.optimization_barrier(feat_cot.transpose(1, 2, 0))
    latent, cot_own = lax.optimization_barrier((latent, cot_own))
    lat_own = lax.optimization_barrier(latent.transpose(1, 0, 2))
    lat_low = lax.ppermute(lat_own[-4:], TILE, up)
    cot_low = lax.ppermute(cot_own[-2:], TILE, up)
    wt = proj_w.T

    stats = call(
        functools.partial(stats_kernel, geometry),
        jax.ShapeDtypeStruct((tokens + 8, 128), F32),
        4,
        (10**8, 10**6),
        "stats",
    )(prompt_ids, hidden, modulation, wt)
    lat_own, cot_own, stats = lax.optimization_barrier((lat_own, cot_own, stats))
    lat_high = lax.ppermute(lat_own[:4], TILE, down)
    cot_high = lax.ppermute(cot_own[:2], TILE, down)
    stats_far = lax.ppermute(stats, "mp", [(0, 1), (1, 0)])

    lat_low, cot_low = lax.optimization_barrier((lat_low, cot_low))
    w1 = dec_w1.transpose(0, 2, 1).reshape(9 * ch, mid)
    slope_two, slope_one = call(
        functools.partial(forward_kernel, geometry),
        (
            jax.ShapeDtypeStruct(((rows + 4) * width, mid), F32),
            jax.ShapeDtypeStruct(((rows + 2) * width, mid), F32),
        ),
        5,
        (8 * 10**9, 8 * 10**6),
        "forward",
        scratch=(
            pltpu.VMEM((3, rows + 8, ch, width), BF),
            pltpu.VMEM((3, (rows + 6) * width, mid), BF),
            pltpu.VMEM(dec_w2.shape, BF),
            pltpu.SemaphoreType.DMA((9,)),
        ),
        smem=0,
        far=1,
        vmem=46,
    )(lat_low, lat_own, lat_high, w1, dec_w2)
    gvt = call(
        functools.partial(backward_kernel, geometry),
        jax.ShapeDtypeStruct((4 * ch, tokens), BF),
        8,
        (7 * 10**9, 8 * 10**6),
        "backward",
        scratch=(
            pltpu.VMEM((3, (rows + 4) * width, mid), BF),
            pltpu.VMEM(((rows + 2) * width, mid), BF),
        ),
    )(step_size, slope_two, slope_one, cot_low, cot_own, cot_high, w1, dec_w2)

    lines = patch + images + 8
    pieces = lax.axis_size("zl")
    high = lines * features // 256
    send, keep = call(
        functools.partial(sums_kernel, width_all, geometry),
        (jax.ShapeDtypeStruct((high, 128), BF), jax.ShapeDtypeStruct((high, 128), F32)),
        7,
        (10**8, 2 * 10**6),
        "sums",
        scratch=(pltpu.VMEM((lines, features), F32),),
    )(prompt_ids, gvt, stats, stats_far, hidden, modulation, wt)
    grad_hidden = call(
        functools.partial(hidden_kernel, width_all, geometry),
        jax.ShapeDtypeStruct((tokens, features), BF),
        7,
        (10**8, 2 * 10**6),
        "grad_hidden",
    )(prompt_ids, gvt, stats, stats_far, hidden, modulation, wt)

    swap = [(0, 1), (1, 0)]
    total = keep + lax.ppermute(send, "core", swap).astype(F32)
    mine, grad_hidden = sum_over_chips(total.reshape(pieces, high // pieces, 128), grad_hidden)
    other = lax.ppermute(mine, "core", swap)

    grad_proj, grad_mod = call(
        functools.partial(last_kernel, images),
        (
            jax.ShapeDtypeStruct((patch, features), F32),
            jax.ShapeDtypeStruct((images, 2, features), F32),
        ),
        3,
        (10**7, 10**6),
        "last",
        scratch=(pltpu.VMEM((2, high, 128), F32),),
        smem=0,
    )(mine, other, wt)
    return (grad_hidden, grad_proj.T, grad_mod)


def solution(mesh):
    fine = Mesh(mesh.devices.reshape(4, 4, 4, 2, 2), ("y", "x", "zl", "core", "mp"))
    return jax.shard_map(
        body,
        mesh=fine,
        in_specs=(
            P(None, TILE, None),
            P(None, TILE, None),
            P(),
            P(),
            P(TILE, "mp"),
            P(None, None, "mp"),
            P(),
            P(),
            P("mp", None),
        ),
        out_specs=(P(TILE, "mp"), P("mp", None), P(None, None, "mp")),
        check_vma=False,
    )
```

```python
import functools

import jax
import jax.numpy as jnp
from jax import lax
from jax.experimental import pallas as pl
from jax.experimental.pallas import tpu as pltpu
from jax.sharding import Mesh, PartitionSpec as P

BF = jnp.bfloat16
F32 = jnp.float32
TILE = ("y", "x", "zl", "core")
OVER_0 = (((0,), (0,)), ((), ()))
OVER_1 = (((1,), (1,)), ((), ()))
WHOLE = pl.BlockSpec(memory_space=pltpu.VMEM)
SCALARS = pl.BlockSpec(memory_space=pltpu.SMEM)


def dot(a, b, dims=(((1,), (0,)), ((), ()))):
    return lax.dot_general(a, b, dims, preferred_element_type=F32)


def before(v, axis):
    place = lax.broadcasted_iota(jnp.int32, v.shape, axis)
    return jnp.where(place == 0, 0.0, pltpu.roll(v, 1, axis))


def after(v, axis):
    n = v.shape[axis]
    place = lax.broadcasted_iota(jnp.int32, v.shape, axis)
    return jnp.where(place == n - 1, 0.0, pltpu.roll(v, n - 1, axis))


def sigmoid(h):
    return 0.5 + 0.5 * jnp.tanh(0.5 * h)


def put_beside(ref, i, v, cols):
    at = pl.ds(i * v.shape[0], v.shape[0])
    ref[0, at, cols] = before(v, 0).astype(BF)
    ref[1, at, cols] = v.astype(BF)
    ref[2, at, cols] = after(v, 0).astype(BF)


def keeper(rows, width, images):
    row_start = place_of(rows, width, images)[1]
    top = jnp.where(row_start > 0, 1.0, 0.0)
    bottom = jnp.where(row_start + rows < width, 1.0, 0.0)

    def masked(v, row):
        return v * top if row < 0 else v * bottom if row >= rows else v

    return masked


def line_of(low, own, high, row):
    if row < 0:
        return low[low.shape[0] + row]
    return own[row] if row < own.shape[0] else high[row - own.shape[0]]


def conv_tile(tap, meanwhile):
    total = None
    for k in range(9):
        part = tap(k)
        total = part if total is None else total + part
        for step in meanwhile[k * len(meanwhile) // 9 : (k + 1) * len(meanwhile) // 9]:
            step()
    return total


def forward_kernel(geometry, lat_low, lat_own, lat_high, w1, w2_far, slope_two, slope_one, lats, acts,
                   w2, sems):
    rows, width, _ = geometry
    loads = [pltpu.make_async_copy(w2_far.at[k], w2.at[k], sems.at[k]) for k in range(9)]
    for load in loads:
        load.start()
    masked = keeper(*geometry)
    for i in range(rows + 8):
        row = i - 4
        v = masked(line_of(lat_low, lat_own, lat_high, row).astype(F32), row)
        lats[0, i] = before(v, 1).astype(BF)
        lats[1, i] = v.astype(BF)
        lats[2, i] = after(v, 1).astype(BF)
    mid = w1.shape[1]
    part_width = mid // 2
    halves = [slice(0, part_width), slice(part_width, mid)]

    def first_layer(i, cols):
        row = i - 3
        taps = [lats[kx, i + ky] for ky in range(3) for kx in range(3)]
        pre = dot(jnp.concatenate(taps, 0), w1[:, cols], OVER_0)
        s = sigmoid(pre)
        if -1 <= row <= rows:
            slope_one[pl.ds((row + 1) * width, width), cols] = s * (1.0 + pre * (1.0 - s))
        put_beside(acts, i, masked((pre * s).astype(BF).astype(F32), row), cols)

    def finish(i, pre, j, cols):
        h = pre[j * width : (j + 1) * width, cols]
        s = sigmoid(h)
        slope_two[pl.ds((i + j) * width, width), cols] = s * (1.0 + h * (1.0 - s))

    per = 4
    for i in range(per + 2):
        for cols in halves:
            first_layer(i, cols)
    steps = []
    for i in range(0, rows + 4, per):
        nexts = [
            functools.partial(first_layer, i + per + 2 + j, cols)
            for j in range(per)
            for cols in halves
            if i + per + 2 + j < rows + 6
        ]

        def tap(k):
            if i == 0:
                loads[k].wait()
            return dot(acts[k % 3, pl.ds((i + k // 3) * width, per * width), :], w2[k], OVER_1)

        pre = conv_tile(tap, nexts + steps)
        steps = [
            functools.partial(finish, i, pre, j, cols) for j in range(per) for cols in halves
        ]
    for step in steps:
        step()


def backward_kernel(geometry, steps, slope_two, slope_one, cot_low, cot_own, cot_high, w1t, w2, out,
                    grads, inner):
    rows, width, _ = geometry
    ch = w1t.shape[0] // 9
    mid = w2.shape[1]
    part_width = mid // 2
    halves = [slice(0, part_width), slice(part_width, mid)]
    masked = keeper(*geometry)
    step = -steps[place_of(*geometry)[0]]

    def second_grad(i, cols):
        cot = line_of(cot_low, cot_own, cot_high, i - 2)[:, cols].astype(F32)
        g = masked(cot * slope_two[pl.ds(i * width, width), cols], i - 2)
        put_beside(grads, i, g.astype(BF).astype(F32), cols)

    taps = []

    def finish(i, back, j, cols):
        at = pl.ds((i + j) * width, width)
        g = back[j * width : (j + 1) * width, cols] * slope_one[at, cols]
        inner[at, cols] = masked(g, i + j - 1).astype(BF)

    per = 5

    def first_taps(i):
        taps.append(dot(w1t[...], inner[pl.ds(i * width, per * width), :], OVER_1))

    for i in range(per + 2):
        for cols in halves:
            second_grad(i, cols)
    todo = []
    for i in range(0, rows + 2, per):
        nexts = [
            functools.partial(second_grad, i + per + 2 + j, cols)
            for j in range(per)
            for cols in halves
            if i + per + 2 + j < rows + 4
        ]

        def tap(k):
            at = pl.ds((i + 2 - k // 3) * width, per * width)
            return dot(grads[2 - k % 3, at, :], w2[k])

        back = conv_tile(tap, nexts + todo)
        todo = [functools.partial(finish, i, back, j, cols) for j in range(per) for cols in halves]
        todo.append(functools.partial(first_taps, i))
    for part in todo:
        part()
    taps = jnp.concatenate(taps, 1)

    lines = []
    for row in range(rows):
        by_kx = []
        for kx in range(3):
            total = None
            for ky in range(3):
                k = 3 * ky + kx
                at = (row + 2 - ky) * width
                part = taps[k * ch : (k + 1) * ch, at : at + width]
                total = part if total is None else total + part
            by_kx.append(total)
        whole = after(by_kx[0], 1) + by_kx[1] + before(by_kx[2], 1)
        lines.append((whole * step).astype(BF))

    half = width // 2
    spot = lax.broadcasted_iota(jnp.int32, (2 * width, 2 * width), 0)
    goal = lax.broadcasted_iota(jnp.int32, (2 * width, 2 * width), 1)
    within = lax.rem(goal, width)
    pick = (lax.div(spot, width) == lax.div(within, half)) & (
        lax.rem(spot, width) == 2 * lax.rem(within, half) + lax.div(goal, width)
    )
    pick = jnp.where(pick, 1.0, 0.0).astype(BF)
    stacked = [
        jnp.concatenate([lines[4 * h + a], lines[4 * h + 2 + a]], 1)
        for h in range(rows // 4)
        for a in range(2)
    ]
    apart = dot(jnp.concatenate(stacked, 0), pick).astype(BF)
    by_tap = jnp.concatenate(
        [
            jnp.concatenate(
                [
                    apart[(2 * h + a) * ch : (2 * h + a + 1) * ch, b * width : (b + 1) * width]
                    for h in range(rows // 4)
                ],
                1,
            )
            for a in range(2)
            for b in range(2)
        ],
        0,
    )
    goal = lax.broadcasted_iota(jnp.int32, (4 * ch, 4 * ch), 0)
    spot = lax.broadcasted_iota(jnp.int32, (4 * ch, 4 * ch), 1)
    order = jnp.where(goal == 4 * lax.rem(spot, ch) + lax.div(spot, ch), 1.0, 0.0).astype(BF)
    out[...] = dot(order, by_tap).astype(BF)


def place_of(rows, width, images):
    tile = 0
    for axis in TILE:
        tile = tile * lax.axis_size(axis) + lax.axis_index(axis)
    row = tile * rows + width // 2
    return lax.rem(lax.div(row, width), images), lax.rem(row, width)


def shift_and_gain(prompt, mod):
    chosen = mod[prompt].astype(F32)
    return chosen[0:1], 1.0 + chosen[1:2]


def in_three(v):
    high = v.astype(BF).astype(F32)
    mid = (v - high).astype(BF).astype(F32)
    return [high, mid, v - high - mid]


def stats_kernel(geometry, prompts, hidden, mod, wt, own, send):
    _, gain = shift_and_gain(prompts[place_of(*geometry)[0]], mod)
    patch, features = wt.shape
    tokens = hidden.shape[0]
    w_gain = (wt[...].astype(F32) * gain).astype(BF)
    states = hidden[...].astype(F32)
    first = jnp.sum(states, axis=1, keepdims=True)
    second = jnp.sum(states * states, axis=1, keepdims=True)
    lane = lax.broadcasted_iota(jnp.int32, (tokens, 128), 1)
    rows = jnp.where(lane == 0, first, jnp.where(lane == 1, second, 0.0)).T
    first, second = rows[0:1], rows[1:2]
    column = jnp.sum(w_gain.astype(F32), axis=1, keepdims=True)
    cross = dot(w_gain, hidden[...], OVER_1) - column * (first / features)
    line = dot(jnp.ones((8, features), BF), w_gain, OVER_1)[0:1]
    line = jnp.concatenate([line, jnp.zeros((1, tokens - patch), F32)], 1)
    none = jnp.zeros((1, tokens), F32)
    own[0:patch, :] = cross
    own[patch:, :] = jnp.concatenate([first, second, line] + [none] * 13, 0)
    send[0:patch, :] = cross.astype(BF)
    parts = in_three(first) + in_three(second) + in_three(line)
    send[patch:, :] = jnp.concatenate(parts + [none] * 7, 0).astype(BF)


def norm_of(width_all, patch, stats, stats_far, hidden):
    own = stats[...]
    far = stats_far[...].astype(F32)
    tokens, half = hidden.shape
    mine = [own[patch + i : patch + i + 1] for i in range(3)]
    theirs = [
        far[patch + 3 * i : patch + 3 * i + 1]
        + far[patch + 3 * i + 1 : patch + 3 * i + 2]
        + far[patch + 3 * i + 2 : patch + 3 * i + 3]
        for i in range(3)
    ]
    mean_val = (mine[0] + theirs[0]) / width_all
    spread = (mine[1] + theirs[1]) / width_all - mean_val * mean_val
    scale = 1.0 / jnp.sqrt(spread + 1e-06)
    apart = [mine[0] / half - mean_val, theirs[0] / half - mean_val]
    rows = [own[0:patch] + far[0:patch], mean_val, scale] + apart
    rows.append(jnp.zeros((128 - patch - 4, tokens), F32))
    turned = jnp.concatenate(rows, 0).T
    mean_val, scale = turned[:, patch : patch + 1], turned[:, patch + 1 : patch + 2]
    w_own, w_far = mine[2][:, 0:patch], theirs[2][:, 0:patch]
    cross = turned[:, 0:patch]
    cross = cross + turned[:, patch + 2 : patch + 3] * w_own + turned[:, patch + 3 : patch + 4] * w_far
    return (hidden[...].astype(F32) - mean_val) * scale, scale, w_own + w_far, cross * scale


def sums_kernel(width_all, geometry, prompts, gvt, stats, stats_far, hidden, mod, wt, send, keep, held):
    patch = gvt.shape[0]
    image, images = place_of(*geometry)[0], geometry[2]
    shift, gain = shift_and_gain(prompts[image], mod)
    normed = norm_of(width_all, patch, stats, stats_far, hidden)[0]
    cross_grad = dot(gvt[...], normed.astype(BF))
    column = jnp.sum(gvt[...].astype(F32), axis=1, keepdims=True)
    held[0:patch, :] = cross_grad * gain + shift * column
    mod_row = jnp.sum(cross_grad * wt[...].astype(F32), axis=0, keepdims=True)
    spot = lax.broadcasted_iota(jnp.int32, (images, mod_row.shape[1]), 0)
    held[patch : patch + images, :] = jnp.where(spot == image, mod_row, 0.0)
    row = dot(jnp.ones((8, gvt.shape[1]), BF), gvt[...], OVER_1)
    held[patch + images :, :] = jnp.zeros((8, mod_row.shape[1]), F32)
    wide = jnp.concatenate([row] * images, 1)
    lane = lax.broadcasted_iota(jnp.int32, wide.shape, 1)
    held[patch + images :, 0 : images * patch] = jnp.where(lax.div(lane, patch) == image, wide, 0.0)
    lines, count = held.shape[0], keep.shape[0] // held.shape[0]
    core = lax.axis_index("core")
    for j in range(count):
        at = pl.ds(j * lines, lines)
        for ref, side in ((keep, core), (send, 1 - core)):
            lanes = pl.ds(pl.multiple_of((side * count + j) * 128, 128), 128)
            ref[at, :] = held[:, lanes].astype(ref.dtype)


def hidden_kernel(width_all, geometry, prompts, gvt, stats, stats_far, hidden, mod, wt, out):
    patch = gvt.shape[0]
    _, gain = shift_and_gain(prompts[place_of(*geometry)[0]], mod)
    normed, scale, w_sum, cross = norm_of(width_all, patch, stats, stats_far, hidden)
    gv = gvt[...].astype(F32).T
    first = jnp.sum(gv * w_sum, axis=1, keepdims=True) / width_all
    second = jnp.sum(gv * cross, axis=1, keepdims=True) / width_all
    grad = dot(gv.astype(BF), wt[...]) * gain
    out[...] = ((grad - first - normed * second) * scale).astype(BF)


def last_kernel(images, mine, other, wt, proj, mod, held):
    patch = wt.shape[0]
    count, piece = mine.shape[0], mine.shape[1]
    lines = patch + images + 8
    core, zl = lax.axis_index("core"), lax.axis_index("zl")
    for d in range(count):
        at = pl.ds(pl.multiple_of(lax.rem(zl + d, count) * piece, 8), piece)
        held[core, at, :] = mine[d].astype(F32)
        held[1 - core, at, :] = other[d].astype(F32)
    blocks = count * piece // lines
    for side in range(2):
        for j in range(blocks):
            at = pl.ds((side * blocks + j) * 128, 128)
            proj[:, at] = held[side, pl.ds(j * lines, patch), :]
            mod[:, 1, at] = held[side, pl.ds(j * lines + patch, images), :]
    sums = []
    for i in range(images):
        j, lane = divmod(i * patch, 128)
        row = held[0, pl.ds(j * lines + patch + images, 1), :]
        sums.append(row[:, lane : lane + patch])
    mod[:, 0, :] = dot(jnp.concatenate(sums, 0).astype(BF), wt[...])


def call(kernel, out_shape, n_in, cost, name, scratch=(), smem=1, far=0, vmem=24):
    return pl.pallas_call(
        kernel,
        out_shape=out_shape,
        in_specs=[SCALARS] * smem + [WHOLE] * (n_in - smem - far) + [pl.BlockSpec(memory_space=pltpu.HBM)] * far,
        out_specs=jax.tree.map(lambda _: WHOLE, out_shape),
        scratch_shapes=list(scratch),
        compiler_params=pltpu.CompilerParams(vmem_limit_bytes=vmem * 2**20),
        cost_estimate=pl.CostEstimate(flops=cost[0], bytes_accessed=cost[1], transcendentals=0),
        name=name,
    )


def sum_over_chips(part, beside):
    count = lax.axis_size("zl")
    zl = lax.axis_index("zl")

    def piece(d):
        return lax.dynamic_index_in_dim(part, lax.rem(zl + d, count), 0, False)

    total = piece(0)
    came = [
        lax.ppermute(piece(d).astype(BF), "zl", [(i, (i + d) % count) for i in range(count)])
        for d in range(1, count)
    ]
    came, beside = lax.optimization_barrier((came, beside))
    for block in came:
        total = total + block.astype(F32)
    plane = ("y", "x")
    chips = lax.axis_size(plane)
    copies = jnp.broadcast_to(total.astype(BF)[None], (chips,) + total.shape)
    total = jnp.sum(lax.all_to_all(copies, plane, 0, 0).astype(F32), axis=0)
    total = lax.optimization_barrier(total).astype(BF)
    came = [
        lax.ppermute(total, "zl", [(i, (i - d) % count) for i in range(count)])
        for d in range(1, count)
    ]
    return jnp.stack([total] + came, 0), beside


def body(feat_cot, latent, dec_w1, dec_w2, hidden, modulation, prompt_ids, step_size, proj_w):
    ch, rows, width = latent.shape
    mid = dec_w2.shape[1]
    images = prompt_ids.shape[0]
    tokens, features = hidden.shape
    patch = proj_w.shape[1]
    width_all = lax.axis_size("mp") * features
    geometry = (rows, width, images)
    count = lax.axis_size(TILE)
    up = [(i, (i + 1) % count) for i in range(count)]
    down = [(b, a) for a, b in up]

    cot_own = lax.optimization_barrier(feat_cot.transpose(1, 2, 0))
    latent, cot_own = lax.optimization_barrier((latent, cot_own))
    lat_own = lax.optimization_barrier(latent.transpose(1, 0, 2))
    lat_low = lax.ppermute(lat_own[-4:], TILE, up)
    cot_low = lax.ppermute(cot_own[-2:], TILE, up)
    wt = proj_w.T

    stats, stats_send = call(
        functools.partial(stats_kernel, geometry),
        (
            jax.ShapeDtypeStruct((patch + 16, tokens), F32),
            jax.ShapeDtypeStruct((patch + 16, tokens), BF),
        ),
        4,
        (10**8, 10**6),
        "stats",
        vmem=54,
    )(prompt_ids, hidden, modulation, wt)
    lat_own, cot_own, stats = lax.optimization_barrier((lat_own, cot_own, stats))
    lat_high = lax.ppermute(lat_own[:4], TILE, down)
    cot_high = lax.ppermute(cot_own[:2], TILE, down)

    lat_low, cot_low = lax.optimization_barrier((lat_low, cot_low))
    w1 = dec_w1.transpose(0, 2, 1).reshape(9 * ch, mid)
    slope_two, slope_one = call(
        functools.partial(forward_kernel, geometry),
        (
            jax.ShapeDtypeStruct(((rows + 4) * width, mid), F32),
            jax.ShapeDtypeStruct(((rows + 2) * width, mid), F32),
        ),
        5,
        (8 * 10**9, 8 * 10**6),
        "forward",
        scratch=(
            pltpu.VMEM((3, rows + 8, ch, width), BF),
            pltpu.VMEM((3, (rows + 6) * width, mid), BF),
            pltpu.VMEM(dec_w2.shape, BF),
            pltpu.SemaphoreType.DMA((9,)),
        ),
        smem=0,
        far=1,
        vmem=46,
    )(lat_low, lat_own, lat_high, w1, dec_w2)
    stats_send, slope_two = lax.optimization_barrier((stats_send, slope_two))
    stats_far = lax.ppermute(stats_send, "mp", [(0, 1), (1, 0)])
    gvt = call(
        functools.partial(backward_kernel, geometry),
        jax.ShapeDtypeStruct((4 * ch, tokens), BF),
        8,
        (7 * 10**9, 8 * 10**6),
        "backward",
        scratch=(
            pltpu.VMEM((3, (rows + 4) * width, mid), BF),
            pltpu.VMEM(((rows + 2) * width, mid), BF),
        ),
    )(step_size, slope_two, slope_one, cot_low, cot_own, cot_high, w1, dec_w2)

    lines = patch + images + 8
    pieces = lax.axis_size("zl")
    high = lines * features // 256
    send, keep = call(
        functools.partial(sums_kernel, width_all, geometry),
        (jax.ShapeDtypeStruct((high, 128), BF), jax.ShapeDtypeStruct((high, 128), F32)),
        7,
        (10**8, 2 * 10**6),
        "sums",
        scratch=(pltpu.VMEM((lines, features), F32),),
    )(prompt_ids, gvt, stats, stats_far, hidden, modulation, wt)
    grad_hidden = call(
        functools.partial(hidden_kernel, width_all, geometry),
        jax.ShapeDtypeStruct((tokens, features), BF),
        7,
        (10**8, 2 * 10**6),
        "grad_hidden",
    )(prompt_ids, gvt, stats, stats_far, hidden, modulation, wt)

    swap = [(0, 1), (1, 0)]
    total = keep + lax.ppermute(send, "core", swap).astype(F32)
    mine, grad_hidden = sum_over_chips(total.reshape(pieces, high // pieces, 128), grad_hidden)
    other = lax.ppermute(mine, "core", swap)

    grad_proj, grad_mod = call(
        functools.partial(last_kernel, images),
        (
            jax.ShapeDtypeStruct((patch, features), F32),
            jax.ShapeDtypeStruct((images, 2, features), F32),
        ),
        3,
        (10**7, 10**6),
        "last",
        scratch=(pltpu.VMEM((2, high, 128), F32),),
        smem=0,
    )(mine, other, wt)
    return (grad_hidden, grad_proj.T, grad_mod)


def solution(mesh):
    fine = Mesh(mesh.devices.reshape(4, 4, 4, 2, 2), ("y", "x", "zl", "core", "mp"))
    return jax.shard_map(
        body,
        mesh=fine,
        in_specs=(
            P(None, TILE, None),
            P(None, TILE, None),
            P(),
            P(),
            P(TILE, "mp"),
            P(None, None, "mp"),
            P(),
            P(),
            P("mp", None),
        ),
        out_specs=(P(TILE, "mp"), P("mp", None), P(None, None, "mp")),
        check_vma=False,
    )
```

```python
import functools

import jax
import jax.numpy as jnp
from jax import lax
from jax.experimental import pallas as pl
from jax.experimental.pallas import tpu as pltpu
from jax.sharding import Mesh, PartitionSpec as P

BF = jnp.bfloat16
F32 = jnp.float32
TILE = ("y", "x", "zl", "core")
OVER_0 = (((0,), (0,)), ((), ()))
OVER_1 = (((1,), (1,)), ((), ()))
WHOLE = pl.BlockSpec(memory_space=pltpu.VMEM)
SCALARS = pl.BlockSpec(memory_space=pltpu.SMEM)


def dot(a, b, dims=(((1,), (0,)), ((), ()))):
    return lax.dot_general(a, b, dims, preferred_element_type=F32)


def before(v, axis):
    place = lax.broadcasted_iota(jnp.int32, v.shape, axis)
    return jnp.where(place == 0, 0.0, pltpu.roll(v, 1, axis))


def after(v, axis):
    n = v.shape[axis]
    place = lax.broadcasted_iota(jnp.int32, v.shape, axis)
    return jnp.where(place == n - 1, 0.0, pltpu.roll(v, n - 1, axis))


def sigmoid(h):
    return 0.5 + 0.5 * jnp.tanh(0.5 * h)


def put_beside(ref, i, v, cols):
    at = pl.ds(i * v.shape[0], v.shape[0])
    ref[0, at, cols] = before(v, 0).astype(BF)
    ref[1, at, cols] = v.astype(BF)
    ref[2, at, cols] = after(v, 0).astype(BF)


def keeper(rows, width, images):
    row_start = place_of(rows, width, images)[1]
    top = jnp.where(row_start > 0, 1.0, 0.0)
    bottom = jnp.where(row_start + rows < width, 1.0, 0.0)

    def masked(v, row):
        return v * top if row < 0 else v * bottom if row >= rows else v

    return masked


def line_of(low, own, high, row):
    if row < 0:
        return low[low.shape[0] + row]
    return own[row] if row < own.shape[0] else high[row - own.shape[0]]


def conv_tile(tap, meanwhile):
    total = None
    for k in range(9):
        part = tap(k)
        total = part if total is None else total + part
        for step in meanwhile[k * len(meanwhile) // 9 : (k + 1) * len(meanwhile) // 9]:
            step()
    return total


def forward_kernel(geometry, lat_low, lat_own, lat_high, w1, w2_far, slope_two, slope_one, lats, acts,
                   w2, sems):
    rows, width, _ = geometry
    loads = [pltpu.make_async_copy(w2_far.at[k], w2.at[k], sems.at[k]) for k in range(9)]
    for load in loads:
        load.start()
    masked = keeper(*geometry)
    for i in range(rows + 8):
        row = i - 4
        v = masked(line_of(lat_low, lat_own, lat_high, row).astype(F32), row)
        lats[0, i] = before(v, 1).astype(BF)
        lats[1, i] = v.astype(BF)
        lats[2, i] = after(v, 1).astype(BF)
    mid = w1.shape[1]
    part_width = mid // 2
    halves = [slice(0, part_width), slice(part_width, mid)]

    def first_layer(i, cols):
        row = i - 3
        taps = [lats[kx, i + ky] for ky in range(3) for kx in range(3)]
        pre = dot(jnp.concatenate(taps, 0), w1[:, cols], OVER_0)
        s = sigmoid(pre)
        if -1 <= row <= rows:
            slope_one[pl.ds((row + 1) * width, width), cols] = s * (1.0 + pre * (1.0 - s))
        put_beside(acts, i, masked((pre * s).astype(BF).astype(F32), row), cols)

    def finish(i, pre, j, cols):
        h = pre[j * width : (j + 1) * width, cols]
        s = sigmoid(h)
        slope_two[pl.ds((i + j) * width, width), cols] = s * (1.0 + h * (1.0 - s))

    per = 4
    for i in range(per + 2):
        for cols in halves:
            first_layer(i, cols)
    steps = []
    for i in range(0, rows + 4, per):
        nexts = [
            functools.partial(first_layer, i + per + 2 + j, cols)
            for j in range(per)
            for cols in halves
            if i + per + 2 + j < rows + 6
        ]

        def tap(k):
            if i == 0:
                loads[k].wait()
            return dot(acts[k % 3, pl.ds((i + k // 3) * width, per * width), :], w2[k], OVER_1)

        pre = conv_tile(tap, nexts + steps)
        steps = [
            functools.partial(finish, i, pre, j, cols) for j in range(per) for cols in halves
        ]
    for step in steps:
        step()


def backward_kernel(geometry, steps, slope_two, slope_one, cot_low, cot_own, cot_high, w1t, w2, out,
                    grads, inner):
    rows, width, _ = geometry
    ch = w1t.shape[0] // 9
    mid = w2.shape[1]
    part_width = mid // 2
    halves = [slice(0, part_width), slice(part_width, mid)]
    masked = keeper(*geometry)
    step = -steps[place_of(*geometry)[0]]

    def second_grad(i, cols):
        cot = line_of(cot_low, cot_own, cot_high, i - 2)[:, cols].astype(F32)
        g = masked(cot * slope_two[pl.ds(i * width, width), cols], i - 2)
        put_beside(grads, i, g.astype(BF).astype(F32), cols)

    taps = []

    def finish(i, back, j, cols):
        at = pl.ds((i + j) * width, width)
        g = back[j * width : (j + 1) * width, cols] * slope_one[at, cols]
        inner[at, cols] = masked(g, i + j - 1).astype(BF)

    per = 5

    def first_taps(i):
        taps.append(dot(w1t[...], inner[pl.ds(i * width, per * width), :], OVER_1))

    for i in range(per + 2):
        for cols in halves:
            second_grad(i, cols)
    todo = []
    for i in range(0, rows + 2, per):
        nexts = [
            functools.partial(second_grad, i + per + 2 + j, cols)
            for j in range(per)
            for cols in halves
            if i + per + 2 + j < rows + 4
        ]

        def tap(k):
            at = pl.ds((i + 2 - k // 3) * width, per * width)
            return dot(grads[2 - k % 3, at, :], w2[k])

        back = conv_tile(tap, nexts + todo)
        todo = [functools.partial(finish, i, back, j, cols) for j in range(per) for cols in halves]
        todo.append(functools.partial(first_taps, i))
    for part in todo:
        part()
    taps = jnp.concatenate(taps, 1)

    lines = []
    for row in range(rows):
        by_kx = []
        for kx in range(3):
            total = None
            for ky in range(3):
                k = 3 * ky + kx
                at = (row + 2 - ky) * width
                part = taps[k * ch : (k + 1) * ch, at : at + width]
                total = part if total is None else total + part
            by_kx.append(total)
        whole = after(by_kx[0], 1) + by_kx[1] + before(by_kx[2], 1)
        lines.append((whole * step).astype(BF))

    half = width // 2
    spot = lax.broadcasted_iota(jnp.int32, (2 * width, 2 * width), 0)
    goal = lax.broadcasted_iota(jnp.int32, (2 * width, 2 * width), 1)
    within = lax.rem(goal, width)
    pick = (lax.div(spot, width) == lax.div(within, half)) & (
        lax.rem(spot, width) == 2 * lax.rem(within, half) + lax.div(goal, width)
    )
    pick = jnp.where(pick, 1.0, 0.0).astype(BF)
    stacked = [
        jnp.concatenate([lines[4 * h + a], lines[4 * h + 2 + a]], 1)
        for h in range(rows // 4)
        for a in range(2)
    ]
    apart = dot(jnp.concatenate(stacked, 0), pick).astype(BF)
    by_tap = jnp.concatenate(
        [
            jnp.concatenate(
                [
                    apart[(2 * h + a) * ch : (2 * h + a + 1) * ch, b * width : (b + 1) * width]
                    for h in range(rows // 4)
                ],
                1,
            )
            for a in range(2)
            for b in range(2)
        ],
        0,
    )
    goal = lax.broadcasted_iota(jnp.int32, (4 * ch, 4 * ch), 0)
    spot = lax.broadcasted_iota(jnp.int32, (4 * ch, 4 * ch), 1)
    order = jnp.where(goal == 4 * lax.rem(spot, ch) + lax.div(spot, ch), 1.0, 0.0).astype(BF)
    out[...] = dot(order, by_tap).astype(BF)


def place_of(rows, width, images):
    tile = 0
    for axis in TILE:
        tile = tile * lax.axis_size(axis) + lax.axis_index(axis)
    row = tile * rows + width // 2
    return lax.rem(lax.div(row, width), images), lax.rem(row, width)


def shift_and_gain(prompt, mod):
    chosen = mod[prompt].astype(F32)
    return chosen[0:1], 1.0 + chosen[1:2]


def in_three(v):
    high = v.astype(BF).astype(F32)
    mid = (v - high).astype(BF).astype(F32)
    return [high, mid, v - high - mid]


def stats_kernel(geometry, prompts, hidden, mod, wt, own, send):
    _, gain = shift_and_gain(prompts[place_of(*geometry)[0]], mod)
    patch, features = wt.shape
    tokens = hidden.shape[0]
    w_gain = (wt[...].astype(F32) * gain).astype(BF)
    states = hidden[...].astype(F32)
    first = jnp.sum(states, axis=1, keepdims=True)
    second = jnp.sum(states * states, axis=1, keepdims=True)
    lane = lax.broadcasted_iota(jnp.int32, (tokens, 128), 1)
    rows = jnp.where(lane == 0, first, jnp.where(lane == 1, second, 0.0)).T
    first, second = rows[0:1], rows[1:2]
    column = jnp.sum(w_gain.astype(F32), axis=1, keepdims=True)
    cross = dot(w_gain, hidden[...], OVER_1) - column * (first / features)
    line = dot(jnp.ones((8, features), BF), w_gain, OVER_1)[0:1]
    line = jnp.concatenate([line, jnp.zeros((1, tokens - patch), F32)], 1)
    none = jnp.zeros((1, tokens), F32)
    own[0:patch, :] = cross
    own[patch:, :] = jnp.concatenate([first, second, line] + [none] * 13, 0)
    send[0:patch, :] = cross.astype(BF)
    parts = in_three(first) + in_three(second) + in_three(line)
    send[patch:, :] = jnp.concatenate(parts + [none] * 7, 0).astype(BF)


def norm_of(width_all, patch, stats, stats_far, hidden):
    own = stats[...]
    far = stats_far[...].astype(F32)
    tokens, half = hidden.shape
    mine = [own[patch + i : patch + i + 1] for i in range(3)]
    theirs = [
        far[patch + 3 * i : patch + 3 * i + 1]
        + far[patch + 3 * i + 1 : patch + 3 * i + 2]
        + far[patch + 3 * i + 2 : patch + 3 * i + 3]
        for i in range(3)
    ]
    mean_val = (mine[0] + theirs[0]) / width_all
    spread = (mine[1] + theirs[1]) / width_all - mean_val * mean_val
    scale = 1.0 / jnp.sqrt(spread + 1e-06)
    apart = [mine[0] / half - mean_val, theirs[0] / half - mean_val]
    rows = [own[0:patch] + far[0:patch], mean_val, scale] + apart
    rows.append(jnp.zeros((128 - patch - 4, tokens), F32))
    turned = jnp.concatenate(rows, 0).T
    mean_val, scale = turned[:, patch : patch + 1], turned[:, patch + 1 : patch + 2]
    w_own, w_far = mine[2][:, 0:patch], theirs[2][:, 0:patch]
    cross = turned[:, 0:patch]
    cross = cross + turned[:, patch + 2 : patch + 3] * w_own + turned[:, patch + 3 : patch + 4] * w_far
    return (hidden[...].astype(F32) - mean_val) * scale, scale, w_own + w_far, cross * scale


def sums_kernel(width_all, geometry, prompts, gvt, stats, stats_far, hidden, mod, wt, send, keep, held):
    patch = gvt.shape[0]
    image, images = place_of(*geometry)[0], geometry[2]
    shift, gain = shift_and_gain(prompts[image], mod)
    normed = norm_of(width_all, patch, stats, stats_far, hidden)[0]
    cross_grad = dot(gvt[...], normed.astype(BF))
    column = jnp.sum(gvt[...].astype(F32), axis=1, keepdims=True)
    held[0:patch, :] = cross_grad * gain + shift * column
    mod_row = jnp.sum(cross_grad * wt[...].astype(F32), axis=0, keepdims=True)
    spot = lax.broadcasted_iota(jnp.int32, (images, mod_row.shape[1]), 0)
    held[patch : patch + images, :] = jnp.where(spot == image, mod_row, 0.0)
    row = dot(jnp.ones((8, gvt.shape[1]), BF), gvt[...], OVER_1)
    held[patch + images :, :] = jnp.zeros((8, mod_row.shape[1]), F32)
    wide = jnp.concatenate([row] * images, 1)
    lane = lax.broadcasted_iota(jnp.int32, wide.shape, 1)
    held[patch + images :, 0 : images * patch] = jnp.where(lax.div(lane, patch) == image, wide, 0.0)
    lines, count = held.shape[0], keep.shape[0] // held.shape[0]
    core = lax.axis_index("core")
    for j in range(count):
        at = pl.ds(j * lines, lines)
        for ref, side in ((keep, core), (send, 1 - core)):
            lanes = pl.ds(pl.multiple_of((side * count + j) * 128, 128), 128)
            ref[at, :] = held[:, lanes].astype(ref.dtype)


def hidden_kernel(width_all, geometry, prompts, gvt, stats, stats_far, hidden, mod, wt, out):
    patch = gvt.shape[0]
    _, gain = shift_and_gain(prompts[place_of(*geometry)[0]], mod)
    normed, scale, w_sum, cross = norm_of(width_all, patch, stats, stats_far, hidden)
    gv = gvt[...].astype(F32).T
    first = jnp.sum(gv * w_sum, axis=1, keepdims=True) / width_all
    second = jnp.sum(gv * cross, axis=1, keepdims=True) / width_all
    grad = dot(gv.astype(BF), wt[...]) * gain
    out[...] = ((grad - first - normed * second) * scale).astype(BF)


def last_kernel(images, mine, other, wt, proj, mod, held):
    patch = wt.shape[0]
    count, piece = mine.shape[0], mine.shape[1]
    lines = patch + images + 8
    core, zl = lax.axis_index("core"), lax.axis_index("zl")
    for d in range(count):
        at = pl.ds(pl.multiple_of(lax.rem(zl + d, count) * piece, 8), piece)
        held[core, at, :] = mine[d].astype(F32)
        held[1 - core, at, :] = other[d].astype(F32)
    blocks = count * piece // lines
    for side in range(2):
        for j in range(blocks):
            at = pl.ds((side * blocks + j) * 128, 128)
            proj[:, at] = held[side, pl.ds(j * lines, patch), :]
            mod[:, 1, at] = held[side, pl.ds(j * lines + patch, images), :]
    sums = []
    for i in range(images):
        j, lane = divmod(i * patch, 128)
        row = held[0, pl.ds(j * lines + patch + images, 1), :]
        sums.append(row[:, lane : lane + patch])
    mod[:, 0, :] = dot(jnp.concatenate(sums, 0).astype(BF), wt[...])


def call(kernel, out_shape, n_in, cost, name, scratch=(), smem=1, far=0, vmem=24):
    return pl.pallas_call(
        kernel,
        out_shape=out_shape,
        in_specs=[SCALARS] * smem + [WHOLE] * (n_in - smem - far) + [pl.BlockSpec(memory_space=pltpu.HBM)] * far,
        out_specs=jax.tree.map(lambda _: WHOLE, out_shape),
        scratch_shapes=list(scratch),
        compiler_params=pltpu.CompilerParams(vmem_limit_bytes=vmem * 2**20),
        cost_estimate=pl.CostEstimate(flops=cost[0], bytes_accessed=cost[1], transcendentals=0),
        name=name,
    )


def sum_over_chips(part, beside):
    count = lax.axis_size("zl")
    zl = lax.axis_index("zl")

    def piece(d):
        return lax.dynamic_index_in_dim(part, lax.rem(zl + d, count), 0, False)

    total = piece(0)
    came = [
        lax.ppermute(piece(d).astype(BF), "zl", [(i, (i + d) % count) for i in range(count)])
        for d in range(1, count)
    ]
    came, beside = lax.optimization_barrier((came, beside))
    for block in came:
        total = total + block.astype(F32)
    plane = ("y", "x")
    chips = lax.axis_size(plane)
    copies = jnp.broadcast_to(total.astype(BF)[None], (chips,) + total.shape)
    total = jnp.sum(lax.all_to_all(copies, plane, 0, 0).astype(F32), axis=0)
    total = lax.optimization_barrier(total).astype(BF)
    came = [
        lax.ppermute(total, "zl", [(i, (i - d) % count) for i in range(count)])
        for d in range(1, count)
    ]
    return jnp.stack([total] + came, 0), beside


def body(feat_cot, latent, dec_w1, dec_w2, hidden, modulation, prompt_ids, step_size, proj_w):
    ch, rows, width = latent.shape
    mid = dec_w2.shape[1]
    images = prompt_ids.shape[0]
    tokens, features = hidden.shape
    patch = proj_w.shape[1]
    width_all = lax.axis_size("mp") * features
    geometry = (rows, width, images)
    count = lax.axis_size(TILE)
    up = [(i, (i + 1) % count) for i in range(count)]
    down = [(b, a) for a, b in up]

    lat_own = lax.optimization_barrier(latent.transpose(1, 0, 2))
    feat_cot, lat_own = lax.optimization_barrier((feat_cot, lat_own))
    lat_low = lax.ppermute(lat_own[-4:], TILE, up)
    lat_high = lax.ppermute(lat_own[:4], TILE, down)
    cot_own = lax.optimization_barrier(feat_cot.transpose(1, 2, 0))
    cot_low = lax.ppermute(cot_own[-2:], TILE, up)
    wt = proj_w.T

    stats, stats_send = call(
        functools.partial(stats_kernel, geometry),
        (
            jax.ShapeDtypeStruct((patch + 16, tokens), F32),
            jax.ShapeDtypeStruct((patch + 16, tokens), BF),
        ),
        4,
        (10**8, 10**6),
        "stats",
        vmem=54,
    )(prompt_ids, hidden, modulation, wt)
    cot_own, stats = lax.optimization_barrier((cot_own, stats))
    cot_high = lax.ppermute(cot_own[:2], TILE, down)

    w1 = dec_w1.transpose(0, 2, 1).reshape(9 * ch, mid)
    slope_two, slope_one = call(
        functools.partial(forward_kernel, geometry),
        (
            jax.ShapeDtypeStruct(((rows + 4) * width, mid), F32),
            jax.ShapeDtypeStruct(((rows + 2) * width, mid), F32),
        ),
        5,
        (8 * 10**9, 8 * 10**6),
        "forward",
        scratch=(
            pltpu.VMEM((3, rows + 8, ch, width), BF),
            pltpu.VMEM((3, (rows + 6) * width, mid), BF),
            pltpu.VMEM(dec_w2.shape, BF),
            pltpu.SemaphoreType.DMA((9,)),
        ),
        smem=0,
        far=1,
        vmem=46,
    )(lat_low, lat_own, lat_high, w1, dec_w2)
    stats_send, slope_two = lax.optimization_barrier((stats_send, slope_two))
    stats_far = lax.ppermute(stats_send, "mp", [(0, 1), (1, 0)])
    gvt = call(
        functools.partial(backward_kernel, geometry),
        jax.ShapeDtypeStruct((4 * ch, tokens), BF),
        8,
        (7 * 10**9, 8 * 10**6),
        "backward",
        scratch=(
            pltpu.VMEM((3, (rows + 4) * width, mid), BF),
            pltpu.VMEM(((rows + 2) * width, mid), BF),
        ),
    )(step_size, slope_two, slope_one, cot_low, cot_own, cot_high, w1, dec_w2)

    lines = patch + images + 8
    pieces = lax.axis_size("zl")
    high = lines * features // 256
    send, keep = call(
        functools.partial(sums_kernel, width_all, geometry),
        (jax.ShapeDtypeStruct((high, 128), BF), jax.ShapeDtypeStruct((high, 128), F32)),
        7,
        (10**8, 2 * 10**6),
        "sums",
        scratch=(pltpu.VMEM((lines, features), F32),),
    )(prompt_ids, gvt, stats, stats_far, hidden, modulation, wt)
    grad_hidden = call(
        functools.partial(hidden_kernel, width_all, geometry),
        jax.ShapeDtypeStruct((tokens, features), BF),
        7,
        (10**8, 2 * 10**6),
        "grad_hidden",
    )(prompt_ids, gvt, stats, stats_far, hidden, modulation, wt)

    swap = [(0, 1), (1, 0)]
    total = keep + lax.ppermute(send, "core", swap).astype(F32)
    mine, grad_hidden = sum_over_chips(total.reshape(pieces, high // pieces, 128), grad_hidden)
    other = lax.ppermute(mine, "core", swap)

    grad_proj, grad_mod = call(
        functools.partial(last_kernel, images),
        (
            jax.ShapeDtypeStruct((patch, features), F32),
            jax.ShapeDtypeStruct((images, 2, features), F32),
        ),
        3,
        (10**7, 10**6),
        "last",
        scratch=(pltpu.VMEM((2, high, 128), F32),),
        smem=0,
    )(mine, other, wt)
    return (grad_hidden, grad_proj.T, grad_mod)


def solution(mesh):
    fine = Mesh(mesh.devices.reshape(4, 4, 4, 2, 2), ("y", "x", "zl", "core", "mp"))
    return jax.shard_map(
        body,
        mesh=fine,
        in_specs=(
            P(None, TILE, None),
            P(None, TILE, None),
            P(),
            P(),
            P(TILE, "mp"),
            P(None, None, "mp"),
            P(),
            P(),
            P("mp", None),
        ),
        out_specs=(P(TILE, "mp"), P("mp", None), P(None, None, "mp")),
        check_vma=False,
    )
```

```python
import functools

import jax
import jax.numpy as jnp
from jax import lax
from jax.experimental import pallas as pl
from jax.experimental.pallas import tpu as pltpu
from jax.sharding import Mesh, PartitionSpec as P

BF = jnp.bfloat16
F32 = jnp.float32
TILE = ("y", "x", "zl", "core")
OVER_0 = (((0,), (0,)), ((), ()))
OVER_1 = (((1,), (1,)), ((), ()))
WHOLE = pl.BlockSpec(memory_space=pltpu.VMEM)
SCALARS = pl.BlockSpec(memory_space=pltpu.SMEM)


def dot(a, b, dims=(((1,), (0,)), ((), ()))):
    return lax.dot_general(a, b, dims, preferred_element_type=F32)


def before(v, axis):
    place = lax.broadcasted_iota(jnp.int32, v.shape, axis)
    return jnp.where(place == 0, 0.0, pltpu.roll(v, 1, axis))


def after(v, axis):
    n = v.shape[axis]
    place = lax.broadcasted_iota(jnp.int32, v.shape, axis)
    return jnp.where(place == n - 1, 0.0, pltpu.roll(v, n - 1, axis))


def sigmoid(h):
    return 0.5 + 0.5 * jnp.tanh(0.5 * h)


def put_beside(ref, i, v, cols):
    at = pl.ds(i * v.shape[0], v.shape[0])
    ref[0, at, cols] = before(v, 0).astype(BF)
    ref[1, at, cols] = v.astype(BF)
    ref[2, at, cols] = after(v, 0).astype(BF)


def keeper(rows, width, images):
    row_start = place_of(rows, width, images)[1]
    top = jnp.where(row_start > 0, 1.0, 0.0)
    bottom = jnp.where(row_start + rows < width, 1.0, 0.0)

    def masked(v, row):
        return v * top if row < 0 else v * bottom if row >= rows else v

    return masked


def line_of(low, own, high, row):
    if row < 0:
        return low[low.shape[0] + row]
    return own[row] if row < own.shape[0] else high[row - own.shape[0]]


def conv_tile(tap, meanwhile):
    total = None
    for k in range(9):
        part = tap(k)
        total = part if total is None else total + part
        for step in meanwhile[k * len(meanwhile) // 9 : (k + 1) * len(meanwhile) // 9]:
            step()
    return total


def forward_kernel(geometry, lat_low, lat_own, lat_high, w1, w2_far, slope_two, slope_one, lats, acts,
                   w2, sems):
    rows, width, _ = geometry
    loads = [pltpu.make_async_copy(w2_far.at[k], w2.at[k], sems.at[k]) for k in range(9)]
    for load in loads:
        load.start()
    masked = keeper(*geometry)
    for i in range(rows + 8):
        row = i - 4
        v = masked(line_of(lat_low, lat_own, lat_high, row).astype(F32), row)
        lats[0, i] = before(v, 1).astype(BF)
        lats[1, i] = v.astype(BF)
        lats[2, i] = after(v, 1).astype(BF)
    mid = w1.shape[1]
    part_width = mid // 2
    halves = [slice(0, part_width), slice(part_width, mid)]

    def first_layer(i, cols):
        row = i - 3
        taps = [lats[kx, i + ky] for ky in range(3) for kx in range(3)]
        pre = dot(jnp.concatenate(taps, 0), w1[:, cols], OVER_0)
        s = sigmoid(pre)
        if -1 <= row <= rows:
            slope_one[pl.ds((row + 1) * width, width), cols] = s * (1.0 + pre * (1.0 - s))
        put_beside(acts, i, masked((pre * s).astype(BF).astype(F32), row), cols)

    def finish(i, pre, j, cols):
        h = pre[j * width : (j + 1) * width, cols]
        s = sigmoid(h)
        slope_two[pl.ds((i + j) * width, width), cols] = s * (1.0 + h * (1.0 - s))

    per = 4
    for i in range(per + 2):
        for cols in halves:
            first_layer(i, cols)
    steps = []
    for i in range(0, rows + 4, per):
        nexts = [
            functools.partial(first_layer, i + per + 2 + j, cols)
            for j in range(per)
            for cols in halves
            if i + per + 2 + j < rows + 6
        ]

        def tap(k):
            if i == 0:
                loads[k].wait()
            return dot(acts[k % 3, pl.ds((i + k // 3) * width, per * width), :], w2[k], OVER_1)

        pre = conv_tile(tap, nexts + steps)
        steps = [
            functools.partial(finish, i, pre, j, cols) for j in range(per) for cols in halves
        ]
    for step in steps:
        step()


def backward_kernel(geometry, steps, slope_two, slope_one, cot_low, cot_own, cot_high, w1t, w2, out,
                    grads, inner):
    rows, width, _ = geometry
    ch = w1t.shape[0] // 9
    mid = w2.shape[1]
    part_width = mid // 2
    halves = [slice(0, part_width), slice(part_width, mid)]
    masked = keeper(*geometry)
    step = -steps[place_of(*geometry)[0]]

    def second_grad(i, cols):
        cot = line_of(cot_low, cot_own, cot_high, i - 2)[:, cols].astype(F32)
        g = masked(cot * slope_two[pl.ds(i * width, width), cols], i - 2)
        put_beside(grads, i, g.astype(BF).astype(F32), cols)

    taps = []

    def finish(i, back, j, cols):
        at = pl.ds((i + j) * width, width)
        g = back[j * width : (j + 1) * width, cols] * slope_one[at, cols]
        inner[at, cols] = masked(g, i + j - 1).astype(BF)

    per = 5

    def first_taps(i):
        taps.append(dot(w1t[...], inner[pl.ds(i * width, per * width), :], OVER_1))

    for i in range(per + 2):
        for cols in halves:
            second_grad(i, cols)
    todo = []
    for i in range(0, rows + 2, per):
        nexts = [
            functools.partial(second_grad, i + per + 2 + j, cols)
            for j in range(per)
            for cols in halves
            if i + per + 2 + j < rows + 4
        ]

        def tap(k):
            at = pl.ds((i + 2 - k // 3) * width, per * width)
            return dot(grads[2 - k % 3, at, :], w2[k])

        back = conv_tile(tap, nexts + todo)
        todo = [functools.partial(finish, i, back, j, cols) for j in range(per) for cols in halves]
        todo.append(functools.partial(first_taps, i))
    for part in todo:
        part()
    taps = jnp.concatenate(taps, 1)

    lines = []
    for row in range(rows):
        by_kx = []
        for kx in range(3):
            total = None
            for ky in range(3):
                k = 3 * ky + kx
                at = (row + 2 - ky) * width
                part = taps[k * ch : (k + 1) * ch, at : at + width]
                total = part if total is None else total + part
            by_kx.append(total)
        whole = after(by_kx[0], 1) + by_kx[1] + before(by_kx[2], 1)
        lines.append((whole * step).astype(BF))

    half = width // 2
    spot = lax.broadcasted_iota(jnp.int32, (2 * width, 2 * width), 0)
    goal = lax.broadcasted_iota(jnp.int32, (2 * width, 2 * width), 1)
    within = lax.rem(goal, width)
    pick = (lax.div(spot, width) == lax.div(within, half)) & (
        lax.rem(spot, width) == 2 * lax.rem(within, half) + lax.div(goal, width)
    )
    pick = jnp.where(pick, 1.0, 0.0).astype(BF)
    stacked = [
        jnp.concatenate([lines[4 * h + a], lines[4 * h + 2 + a]], 1)
        for h in range(rows // 4)
        for a in range(2)
    ]
    apart = dot(jnp.concatenate(stacked, 0), pick).astype(BF)
    by_tap = jnp.concatenate(
        [
            jnp.concatenate(
                [
                    apart[(2 * h + a) * ch : (2 * h + a + 1) * ch, b * width : (b + 1) * width]
                    for h in range(rows // 4)
                ],
                1,
            )
            for a in range(2)
            for b in range(2)
        ],
        0,
    )
    goal = lax.broadcasted_iota(jnp.int32, (4 * ch, 4 * ch), 0)
    spot = lax.broadcasted_iota(jnp.int32, (4 * ch, 4 * ch), 1)
    order = jnp.where(goal == 4 * lax.rem(spot, ch) + lax.div(spot, ch), 1.0, 0.0).astype(BF)
    out[...] = dot(order, by_tap).astype(BF)


def place_of(rows, width, images):
    tile = 0
    for axis in TILE:
        tile = tile * lax.axis_size(axis) + lax.axis_index(axis)
    row = tile * rows + width // 2
    return lax.rem(lax.div(row, width), images), lax.rem(row, width)


def shift_and_gain(prompt, mod):
    chosen = mod[prompt].astype(F32)
    return chosen[0:1], 1.0 + chosen[1:2]


def in_three(v):
    high = v.astype(BF).astype(F32)
    mid = (v - high).astype(BF).astype(F32)
    return [high, mid, v - high - mid]


def stats_kernel(geometry, prompts, hidden, mod, wt, own, send):
    _, gain = shift_and_gain(prompts[place_of(*geometry)[0]], mod)
    patch, features = wt.shape
    tokens = hidden.shape[0]
    w_gain = (wt[...].astype(F32) * gain).astype(BF)
    states = hidden[...].astype(F32)
    first = jnp.sum(states, axis=1, keepdims=True)
    second = jnp.sum(states * states, axis=1, keepdims=True)
    lane = lax.broadcasted_iota(jnp.int32, (tokens, 128), 1)
    rows = jnp.where(lane == 0, first, jnp.where(lane == 1, second, 0.0)).T
    first, second = rows[0:1], rows[1:2]
    column = jnp.sum(w_gain.astype(F32), axis=1, keepdims=True)
    cross = dot(w_gain, hidden[...], OVER_1) - column * (first / features)
    line = dot(jnp.ones((8, features), BF), w_gain, OVER_1)[0:1]
    line = jnp.concatenate([line, jnp.zeros((1, tokens - patch), F32)], 1)
    none = jnp.zeros((1, tokens), F32)
    own[0:patch, :] = cross
    own[patch:, :] = jnp.concatenate([first, second, line] + [none] * 13, 0)
    send[0:patch, :] = cross.astype(BF)
    parts = in_three(first) + in_three(second) + in_three(line)
    send[patch:, :] = jnp.concatenate(parts + [none] * 7, 0).astype(BF)


def norm_of(width_all, patch, stats, stats_far, hidden):
    own = stats[...]
    far = stats_far[...].astype(F32)
    tokens, half = hidden.shape
    mine = [own[patch + i : patch + i + 1] for i in range(3)]
    theirs = [
        far[patch + 3 * i : patch + 3 * i + 1]
        + far[patch + 3 * i + 1 : patch + 3 * i + 2]
        + far[patch + 3 * i + 2 : patch + 3 * i + 3]
        for i in range(3)
    ]
    mean_val = (mine[0] + theirs[0]) / width_all
    spread = (mine[1] + theirs[1]) / width_all - mean_val * mean_val
    scale = 1.0 / jnp.sqrt(spread + 1e-06)
    apart = [mine[0] / half - mean_val, theirs[0] / half - mean_val]
    rows = [own[0:patch] + far[0:patch], mean_val, scale] + apart
    rows.append(jnp.zeros((128 - patch - 4, tokens), F32))
    turned = jnp.concatenate(rows, 0).T
    mean_val, scale = turned[:, patch : patch + 1], turned[:, patch + 1 : patch + 2]
    w_own, w_far = mine[2][:, 0:patch], theirs[2][:, 0:patch]
    cross = turned[:, 0:patch]
    cross = cross + turned[:, patch + 2 : patch + 3] * w_own + turned[:, patch + 3 : patch + 4] * w_far
    return (hidden[...].astype(F32) - mean_val) * scale, scale, w_own + w_far, cross * scale


def sums_kernel(width_all, geometry, prompts, gvt, stats, stats_far, hidden, mod, wt, send, keep, held):
    patch = gvt.shape[0]
    image, images = place_of(*geometry)[0], geometry[2]
    shift, gain = shift_and_gain(prompts[image], mod)
    normed = norm_of(width_all, patch, stats, stats_far, hidden)[0]
    cross_grad = dot(gvt[...], normed.astype(BF))
    column = jnp.sum(gvt[...].astype(F32), axis=1, keepdims=True)
    held[0:patch, :] = cross_grad * gain + shift * column
    mod_row = jnp.sum(cross_grad * wt[...].astype(F32), axis=0, keepdims=True)
    spot = lax.broadcasted_iota(jnp.int32, (images, mod_row.shape[1]), 0)
    held[patch : patch + images, :] = jnp.where(spot == image, mod_row, 0.0)
    row = dot(jnp.ones((8, gvt.shape[1]), BF), gvt[...], OVER_1)
    held[patch + images :, :] = jnp.zeros((8, mod_row.shape[1]), F32)
    wide = jnp.concatenate([row] * images, 1)
    lane = lax.broadcasted_iota(jnp.int32, wide.shape, 1)
    held[patch + images :, 0 : images * patch] = jnp.where(lax.div(lane, patch) == image, wide, 0.0)
    lines, count = held.shape[0], keep.shape[0] // held.shape[0]
    core = lax.axis_index("core")
    for j in range(count):
        at = pl.ds(j * lines, lines)
        for ref, side in ((keep, core), (send, 1 - core)):
            lanes = pl.ds(pl.multiple_of((side * count + j) * 128, 128), 128)
            ref[at, :] = held[:, lanes].astype(ref.dtype)


def hidden_kernel(width_all, geometry, prompts, gvt, stats, stats_far, hidden, mod, wt, out):
    patch = gvt.shape[0]
    _, gain = shift_and_gain(prompts[place_of(*geometry)[0]], mod)
    normed, scale, w_sum, cross = norm_of(width_all, patch, stats, stats_far, hidden)
    gv = gvt[...].astype(F32).T
    first = jnp.sum(gv * w_sum, axis=1, keepdims=True) / width_all
    second = jnp.sum(gv * cross, axis=1, keepdims=True) / width_all
    grad = dot(gv.astype(BF), wt[...]) * gain
    out[...] = ((grad - first - normed * second) * scale).astype(BF)


def last_kernel(images, mine, other, wt, proj, mod, held):
    patch = wt.shape[0]
    count, piece = mine.shape[0], mine.shape[1]
    lines = patch + images + 8
    core, zl = lax.axis_index("core"), lax.axis_index("zl")
    for d in range(count):
        at = pl.ds(pl.multiple_of(lax.rem(zl + d, count) * piece, 8), piece)
        held[core, at, :] = mine[d].astype(F32)
        held[1 - core, at, :] = other[d].astype(F32)
    blocks = count * piece // lines
    for side in range(2):
        for j in range(blocks):
            at = pl.ds((side * blocks + j) * 128, 128)
            proj[:, at] = held[side, pl.ds(j * lines, patch), :]
            mod[:, 1, at] = held[side, pl.ds(j * lines + patch, images), :]
    sums = []
    for i in range(images):
        j, lane = divmod(i * patch, 128)
        row = held[0, pl.ds(j * lines + patch + images, 1), :]
        sums.append(row[:, lane : lane + patch])
    mod[:, 0, :] = dot(jnp.concatenate(sums, 0).astype(BF), wt[...])


def call(kernel, out_shape, n_in, cost, name, scratch=(), smem=1, far=0, vmem=24):
    return pl.pallas_call(
        kernel,
        out_shape=out_shape,
        in_specs=[SCALARS] * smem + [WHOLE] * (n_in - smem - far) + [pl.BlockSpec(memory_space=pltpu.HBM)] * far,
        out_specs=jax.tree.map(lambda _: WHOLE, out_shape),
        scratch_shapes=list(scratch),
        compiler_params=pltpu.CompilerParams(vmem_limit_bytes=vmem * 2**20),
        cost_estimate=pl.CostEstimate(flops=cost[0], bytes_accessed=cost[1], transcendentals=0),
        name=name,
    )


def sum_over_chips(part, beside):
    count = lax.axis_size("zl")
    zl = lax.axis_index("zl")

    def piece(d):
        return lax.dynamic_index_in_dim(part, lax.rem(zl + d, count), 0, False)

    total = piece(0)
    came = [
        lax.ppermute(piece(d).astype(BF), "zl", [(i, (i + d) % count) for i in range(count)])
        for d in range(1, count)
    ]
    came, beside = lax.optimization_barrier((came, beside))
    for block in came:
        total = total + block.astype(F32)
    for axis in ("x", "y"):
        size = lax.axis_size(axis)
        out = total.astype(BF)
        came = [
            lax.ppermute(out, axis, [(i, (i + d) % size) for i in range(size)])
            for d in range(1, size)
        ]
        for block in came:
            total = total + block.astype(F32)
    total = lax.optimization_barrier(total).astype(BF)
    came = [
        lax.ppermute(total, "zl", [(i, (i - d) % count) for i in range(count)])
        for d in range(1, count)
    ]
    return jnp.stack([total] + came, 0), beside


def body(feat_cot, latent, dec_w1, dec_w2, hidden, modulation, prompt_ids, step_size, proj_w):
    ch, rows, width = latent.shape
    mid = dec_w2.shape[1]
    images = prompt_ids.shape[0]
    tokens, features = hidden.shape
    patch = proj_w.shape[1]
    width_all = lax.axis_size("mp") * features
    geometry = (rows, width, images)
    count = lax.axis_size(TILE)
    up = [(i, (i + 1) % count) for i in range(count)]
    down = [(b, a) for a, b in up]

    lat_own = lax.optimization_barrier(latent.transpose(1, 0, 2))
    feat_cot, lat_own = lax.optimization_barrier((feat_cot, lat_own))
    lat_low = lax.ppermute(lat_own[-4:], TILE, up)
    lat_high = lax.ppermute(lat_own[:4], TILE, down)
    cot_own = lax.optimization_barrier(feat_cot.transpose(1, 2, 0))
    cot_low = lax.ppermute(cot_own[-2:], TILE, up)
    wt = proj_w.T

    stats, stats_send = call(
        functools.partial(stats_kernel, geometry),
        (
            jax.ShapeDtypeStruct((patch + 16, tokens), F32),
            jax.ShapeDtypeStruct((patch + 16, tokens), BF),
        ),
        4,
        (10**8, 10**6),
        "stats",
        vmem=54,
    )(prompt_ids, hidden, modulation, wt)
    cot_own, stats = lax.optimization_barrier((cot_own, stats))
    cot_high = lax.ppermute(cot_own[:2], TILE, down)

    w1 = dec_w1.transpose(0, 2, 1).reshape(9 * ch, mid)
    slope_two, slope_one = call(
        functools.partial(forward_kernel, geometry),
        (
            jax.ShapeDtypeStruct(((rows + 4) * width, mid), F32),
            jax.ShapeDtypeStruct(((rows + 2) * width, mid), F32),
        ),
        5,
        (8 * 10**9, 8 * 10**6),
        "forward",
        scratch=(
            pltpu.VMEM((3, rows + 8, ch, width), BF),
            pltpu.VMEM((3, (rows + 6) * width, mid), BF),
            pltpu.VMEM(dec_w2.shape, BF),
            pltpu.SemaphoreType.DMA((9,)),
        ),
        smem=0,
        far=1,
        vmem=46,
    )(lat_low, lat_own, lat_high, w1, dec_w2)
    stats_send, slope_two = lax.optimization_barrier((stats_send, slope_two))
    stats_far = lax.ppermute(stats_send, "mp", [(0, 1), (1, 0)])
    gvt = call(
        functools.partial(backward_kernel, geometry),
        jax.ShapeDtypeStruct((4 * ch, tokens), BF),
        8,
        (7 * 10**9, 8 * 10**6),
        "backward",
        scratch=(
            pltpu.VMEM((3, (rows + 4) * width, mid), BF),
            pltpu.VMEM(((rows + 2) * width, mid), BF),
        ),
    )(step_size, slope_two, slope_one, cot_low, cot_own, cot_high, w1, dec_w2)

    lines = patch + images + 8
    pieces = lax.axis_size("zl")
    high = lines * features // 256
    send, keep = call(
        functools.partial(sums_kernel, width_all, geometry),
        (jax.ShapeDtypeStruct((high, 128), BF), jax.ShapeDtypeStruct((high, 128), F32)),
        7,
        (10**8, 2 * 10**6),
        "sums",
        scratch=(pltpu.VMEM((lines, features), F32),),
    )(prompt_ids, gvt, stats, stats_far, hidden, modulation, wt)
    grad_hidden = call(
        functools.partial(hidden_kernel, width_all, geometry),
        jax.ShapeDtypeStruct((tokens, features), BF),
        7,
        (10**8, 2 * 10**6),
        "grad_hidden",
    )(prompt_ids, gvt, stats, stats_far, hidden, modulation, wt)

    swap = [(0, 1), (1, 0)]
    total = keep + lax.ppermute(send, "core", swap).astype(F32)
    mine, grad_hidden = sum_over_chips(total.reshape(pieces, high // pieces, 128), grad_hidden)
    other = lax.ppermute(mine, "core", swap)

    grad_proj, grad_mod = call(
        functools.partial(last_kernel, images),
        (
            jax.ShapeDtypeStruct((patch, features), F32),
            jax.ShapeDtypeStruct((images, 2, features), F32),
        ),
        3,
        (10**7, 10**6),
        "last",
        scratch=(pltpu.VMEM((2, high, 128), F32),),
        smem=0,
    )(mine, other, wt)
    return (grad_hidden, grad_proj.T, grad_mod)


def solution(mesh):
    fine = Mesh(mesh.devices.reshape(4, 4, 4, 2, 2), ("y", "x", "zl", "core", "mp"))
    return jax.shard_map(
        body,
        mesh=fine,
        in_specs=(
            P(None, TILE, None),
            P(None, TILE, None),
            P(),
            P(),
            P(TILE, "mp"),
            P(None, None, "mp"),
            P(),
            P(),
            P("mp", None),
        ),
        out_specs=(P(TILE, "mp"), P("mp", None), P(None, None, "mp")),
        check_vma=False,
    )
```
